32 devices in a mesh: grp: 2 (over y), col: 4 (over z), row: 2 (over x), limb: 2 (over core).
Axes of the slice: x: 2, y: 2, z: 4, core: 2. Of those that a mesh axis runs over, the one named last changes fastest.
Arguments:
- database: bfloat16 [8192, 8192], P(('grp', 'row'), 'col'), parts along dimension 0, may hold values from -128 to 127, as said below
- lwe_matrix: bfloat16 [8192, 2, 512], P('col', 'limb'), may hold values from -0.0008544922 to 0.0008544922
- secret_ct: float32 [2, 2, 2, 512, 4096], P(None, None, 'limb', 'col', 'row'), may hold values from -6 to 6
Outputs:
- encrypted_product: float32 [4, 2, 4096], P('grp', None, 'row'), parts along dimension 0
The draws below stay inside these ranges and needn't reach their ends.
There are 2 independent parts, one for each index of `grp`. The reference program is written for one: setup_inputs(seed, part) draws one part's arguments, and reference() takes and returns one part's arrays. A program takes and returns all parts, laid end to end along the dimension named above; an argument that names none is the same for every part. Nothing has to cross between parts.
Inputs may be any that keep to these rules, and one draw needn't show every extreme that they name: `database`: whole numbers.
All inputs are finite; a program needn't handle non-finite values.
Results may differ from the reference program's by a relative error of at most 0.0003.
Values sent between devices are 32-bit elements; how exact they have to be, the bound alone decides.
No kernel may reach another device: no remote copies, remote signals or barrier semaphores. Data moves between devices by JAX's collectives and lax.ppermute only.
A program may use at most 64 MiB of HBM per device.

```python
import math
import jax
import jax.numpy as jnp
from jax import lax

DEGREE = 4096
HALF = 512
COLUMNS = 8192
N_ROW = 2


def draw_database(key, part):
    values = jax.random.randint(key, (DEGREE, COLUMNS), -128, 128)
    return values.astype(jnp.float32).astype(jnp.bfloat16)


def level_of(stream_key, extent, shards, smallest, largest):
    def one(axis_at, blocks):
        heights = jax.random.uniform(jax.random.fold_in(jax.random.fold_in(stream_key, 6), axis_at), (blocks,), jnp.float32, smallest / len(shards), largest / len(shards))
        return jnp.repeat(jnp.exp(heights), extent[axis_at] // blocks).reshape((-1,) + (1,) * (len(extent) - axis_at - 1))

    factor_of = one(*shards[0])
    for cut in shards[1:]:
        factor_of = factor_of * one(*cut)
    return factor_of


def noise(stream_key, extent, scale, reach, pieces=(), held_as=jnp.bfloat16):
    gain = level_of(stream_key, extent, pieces, -0.22, 0.18) if pieces else 1.0
    result = jax.random.normal(stream_key, extent, jnp.float32) * scale * gain
    return jnp.minimum(jnp.maximum(result, -reach), reach).astype(held_as)


def setup_inputs(seed: int = 0, part: int = 0) -> dict:
    seeds = jax.random.split(jax.random.key(seed), 4)
    part_splits = jax.random.split(jax.random.fold_in(seeds[3], part), 4)
    return {
        "database": draw_database(jax.random.fold_in(jax.random.fold_in(seeds[3], part), 71), part),
        "lwe_matrix": noise(seeds[1], (COLUMNS, 2, HALF), (COLUMNS * 5461) ** -0.5, 0.0008544922, ((0, 4), (1, 2))),
        "secret_ct": noise(seeds[2], (2, 2, 2, HALF, DEGREE), 1.0, 6.0, ((2, 2), (3, 4), (4, 2)), jnp.float32),
    }


def reference(database, lwe_matrix, secret_ct):
    hint_full = jnp.dot(database, lwe_matrix.reshape(COLUMNS, 2 * HALF), preferred_element_type=jnp.float32)
    row_index = jnp.arange(DEGREE).astype(hint_full.dtype)
    twist_factor = jnp.exp(-1j * jnp.pi * row_index / DEGREE)
    spectrum = jnp.fft.fft(hint_full * twist_factor[:, None], axis=0) / math.sqrt(DEGREE)
    spectrum = spectrum.reshape(DEGREE // N_ROW, N_ROW, 2 * HALF).transpose(1, 0, 2).reshape(DEGREE, 2 * HALF)
    real_part = jnp.real(spectrum).T
    imag_part = jnp.imag(spectrum).T
    cipher = secret_ct.reshape(2, 2, 2 * HALF, DEGREE)
    out_real = lax.optimization_barrier(jnp.sum(real_part * cipher[:, 0] - imag_part * cipher[:, 1], axis=1))
    out_imag = lax.optimization_barrier(jnp.sum(real_part * cipher[:, 1] + imag_part * cipher[:, 0], axis=1))
    return jnp.stack([out_real, out_imag], axis=1) / math.sqrt(2 * HALF)
```

```python
import functools
import math

import jax
import jax.numpy as jnp
import numpy as np
from jax import lax
from jax.experimental import pallas as pl
from jax.experimental.pallas import tpu as pltpu
from jax.sharding import PartitionSpec as P

LANES = 128
MIB = 1 << 20


def split_bf16(x):
    high = x.astype(jnp.bfloat16)
    low = (x - high.astype(jnp.float32)).astype(jnp.bfloat16)
    return high, low


def hint_kernel(groups, parts, block, lwe_ref, data_ref, *rest):
    outs, turned = rest[:-1], rest[-1]

    @pl.when(pl.program_id(0) == 0)
    def _():
        turned[...] = lwe_ref[...].T

    for g in range(groups):
        rows = slice(g * parts * block, (g + 1) * parts * block)
        res = lax.dot_general(
            turned[rows, :], data_ref[...], (((1,), (1,)), ((), ())), preferred_element_type=jnp.float32
        )
        for k in range(parts):
            outs[k][g * block : (g + 1) * block, :] = res[k * block : (k + 1) * block, :]


def partial_hint(lwe, database, groups, parts):
    depth, columns = lwe.shape
    rows = database.shape[0]
    block = columns // (groups * parts)
    tile = min(256, rows)
    return pl.pallas_call(
        functools.partial(hint_kernel, groups, parts, block),
        grid=(rows // tile,),
        in_specs=[
            pl.BlockSpec((depth, columns), lambda i: (0, 0)),
            pl.BlockSpec((tile, depth), lambda i: (i, 0)),
        ],
        out_specs=[pl.BlockSpec((groups * block, tile), lambda i: (0, i))] * parts,
        out_shape=[jax.ShapeDtypeStruct((groups * block, rows), jnp.float32)] * parts,
        scratch_shapes=[pltpu.VMEM((columns, depth), jnp.bfloat16)],
        compiler_params=pltpu.CompilerParams(vmem_limit_bytes=48 * MIB),
        cost_estimate=pl.CostEstimate(
            flops=2 * rows * depth * columns, bytes_accessed=2 * rows * depth, transcendentals=0
        ),
    )(lwe, database)


def fft_list(re, im):
    n = len(re)
    if n == 1:
        return re, im
    er, ei = fft_list(re[0::2], im[0::2])
    odd_r, odd_i = fft_list(re[1::2], im[1::2])
    half = n // 2
    out_r, out_i = [None] * n, [None] * n
    for k in range(half):
        xr, xi = odd_r[k], odd_i[k]
        if k == 0:
            tr, ti = xr, xi
        elif 4 * k == n:
            tr, ti = xi, -xr
        elif 8 * k == n:
            c = math.sqrt(0.5)
            tr, ti = (xr + xi) * c, (xi - xr) * c
        elif 8 * k == 3 * n:
            c = math.sqrt(0.5)
            tr, ti = (xi - xr) * c, -(xr + xi) * c
        else:
            c, s = math.cos(2 * math.pi * k / n), math.sin(2 * math.pi * k / n)
            tr, ti = xr * c + xi * s, xi * c - xr * s
        out_r[k], out_i[k] = er[k] + tr, ei[k] + ti
        out_r[k + half], out_i[k + half] = er[k] - tr, ei[k] - ti
    return out_r, out_i


def transform_kernel(blocks, radix, rows, *refs):
    hints = refs[:blocks]
    first_ref, twist_ref, table_hi, table_lo, cipher_ref, out_ref, stage = refs[blocks:]
    for top in range(0, rows, 8):
        re, im = [], []
        for u in range(radix):
            lanes = slice(u * LANES, (u + 1) * LANES)
            real = imag = None
            for b in range(blocks):
                h = hints[b][top : top + 8, lanes]
                x, y = h * first_ref[2 * b : 2 * b + 1, lanes], h * first_ref[2 * b + 1 : 2 * b + 2, lanes]
                real = x if real is None else real + x
                imag = y if imag is None else imag + y
            re.append(real)
            im.append(imag)
        re, im = fft_list(re, im)
        for r in range(radix):
            c = twist_ref[2 * r : 2 * r + 1, :]
            s = twist_ref[2 * r + 1 : 2 * r + 2, :]
            at = slice(r * rows + top, r * rows + top + 8)
            stage[at, :LANES] = re[r] * c + im[r] * s
            stage[at, LANES:] = im[r] * c - re[r] * s
    for r in range(radix):
        high, low = split_bf16(stage[r * rows : (r + 1) * rows, :])
        dot = functools.partial(jnp.dot, preferred_element_type=jnp.float32)
        spec = dot(high, table_hi[...]) + (dot(low, table_hi[...]) + dot(high, table_lo[...]))
        sr, si = spec[:, :LANES], spec[:, LANES:]
        lanes = slice(r * LANES, (r + 1) * LANES)
        for c in range(2):
            a, b = cipher_ref[2 * c, :, lanes], cipher_ref[2 * c + 1, :, lanes]
            out_ref[2 * c : 2 * c + 1, lanes] = jnp.sum(sr * a - si * b, axis=0, keepdims=True)
            out_ref[2 * c + 1 : 2 * c + 2, lanes] = jnp.sum(sr * b + si * a, axis=0, keepdims=True)


def transform_products(hints, first, twist, tables, cipher, part):
    rows, points = hints[0].shape
    radix = points // LANES
    whole = lambda a: pl.BlockSpec(a.shape, lambda i: (0,) * a.ndim)
    return pl.pallas_call(
        functools.partial(transform_kernel, len(hints), radix, rows),
        grid=(1,),
        in_specs=[whole(h) for h in hints]
        + [whole(first), whole(twist), whole(tables[0]), whole(tables[1])]
        + [pl.BlockSpec((4, rows, points), lambda i: (0, part, 0))],
        out_specs=pl.BlockSpec((4, points), lambda i: (0, 0)),
        out_shape=jax.ShapeDtypeStruct((4, points), jnp.float32),
        scratch_shapes=[pltpu.VMEM((radix * rows, 2 * LANES), jnp.float32)],
        compiler_params=pltpu.CompilerParams(vmem_limit_bytes=32 * MIB),
        cost_estimate=pl.CostEstimate(
            flops=6 * radix * rows * 256 * 256, bytes_accessed=24 * rows * points, transcendentals=0
        ),
    )(*hints, first, twist, *tables, cipher)


def xor_pairs(size, step):
    return [(i, i ^ step) for i in range(size)]


def sum_over(x, axes):
    for axis in axes:
        size = lax.axis_size(axis)
        if size & (size - 1):
            x = lax.psum(x, axis)
            continue
        step = 1
        while step < size:
            x = x + lax.ppermute(x, axis, xor_pairs(size, step))
            step *= 2
    return x


def body(parts, database, lwe_matrix, secret_ct):
    row_count, row_rank = lax.axis_size("row"), lax.axis_index("row")
    col_count = lax.axis_size("col")
    points = database.shape[0]
    degree = points * row_count
    radix = points // LANES
    own = secret_ct.shape[3]

    cipher = secret_ct.reshape(4, own, LANES, radix).swapaxes(2, 3).reshape(4, own, points)

    source = (row_rank + jnp.arange(row_count, dtype=jnp.int32)) % row_count if row_count == 2 else jnp.arange(row_count, dtype=jnp.int32)
    index = (source[:, None] * points + jnp.arange(points, dtype=jnp.int32)[None, :]) * (2 * row_rank + 1) % (2 * degree)
    angle = index.astype(jnp.float32) * (np.pi / degree)
    first = jnp.stack([jnp.cos(angle), -jnp.sin(angle)], axis=1).reshape(2 * row_count, points)
    lane = np.arange(LANES)
    turn = 2 * np.pi * (np.arange(radix)[:, None] * lane[None, :] % points) / points
    twist = jnp.asarray(np.stack([np.cos(turn), np.sin(turn)], axis=1).reshape(2 * radix, LANES), jnp.float32)
    small = 2 * np.pi * (lane[:, None] * lane[None, :] % LANES) / LANES
    table = np.block([[np.cos(small), -np.sin(small)], [np.sin(small), np.cos(small)]]).astype(np.float32)
    high = table.astype(jnp.bfloat16)
    low = (table - high.astype(np.float32)).astype(jnp.bfloat16)
    tables = (jnp.asarray(high), jnp.asarray(low))

    partial = partial_hint(lwe_matrix[:, 0, :], database, col_count, parts)
    total = None
    for k in range(parts):
        mine = lax.psum_scatter(partial[k], "col", scatter_dimension=0, tiled=True)
        if row_count == 2:
            hints = [mine, lax.ppermute(mine, "row", [(0, 1), (1, 0)])]
        else:
            gathered = lax.all_gather(mine, "row")
            hints = [gathered[b] for b in range(row_count)]
        part = transform_products(hints, first, twist, tables, cipher, k)
        total = part if total is None else total + part
    total = sum_over(total, ("limb", "col"))
    scale = 1.0 / (math.sqrt(degree) * math.sqrt(2 * lwe_matrix.shape[2]))
    total = total.reshape(4, radix, LANES).swapaxes(1, 2).reshape(2, 2, points)
    return total * scale


def solution(mesh):
    placed = (P(("grp", "row"), "col"), P("col", "limb", None), P(None, None, "limb", "col", "row"))

    def whole(database, lwe_matrix, secret_ct):
        own = lwe_matrix.shape[2] // mesh.shape["col"]
        parts = 2 if own % 16 == 0 else 1
        return jax.shard_map(
            functools.partial(body, parts), mesh=mesh, in_specs=placed, out_specs=P("grp", None, "row"), check_vma=False
        )(database, lwe_matrix, secret_ct)

    return whole
```

```python
import functools
import math

import jax
import jax.numpy as jnp
import numpy as np
from jax import lax
from jax.experimental import pallas as pl
from jax.experimental.pallas import tpu as pltpu
from jax.sharding import PartitionSpec as P

LANES = 128
MIB = 1 << 20
SWAP = [(0, 1), (1, 0)]
NEIGHBOURS = [(0, 1), (1, 0), (2, 3), (3, 2)]
END_TO_FAR_MIDDLE = [(0, 2), (3, 1)]
CROSS = [(1, 2), (2, 1)]
ROUND = [(0, 1), (1, 3), (3, 2), (2, 0)]


def split_bf16(x):
    high = x.astype(jnp.bfloat16)
    low = (x - high.astype(jnp.float32)).astype(jnp.bfloat16)
    return high, low


def hint_kernel(groups, parts, block, lwe_ref, data_ref, *rest):
    outs, turned = rest[:-1], rest[-1]

    @pl.when(pl.program_id(0) == 0)
    def _():
        turned[...] = lwe_ref[...].T

    for g in range(groups):
        rows = slice(g * parts * block, (g + 1) * parts * block)
        res = lax.dot_general(
            turned[rows, :], data_ref[...], (((1,), (1,)), ((), ())), preferred_element_type=jnp.float32
        )
        for k in range(parts):
            outs[k][g * block : (g + 1) * block, :] = res[k * block : (k + 1) * block, :]


def partial_hint(lwe, database, groups, parts):
    depth, columns = lwe.shape
    rows = database.shape[0]
    block = columns // (groups * parts)
    tile = min(256, rows)
    return pl.pallas_call(
        functools.partial(hint_kernel, groups, parts, block),
        grid=(rows // tile,),
        in_specs=[
            pl.BlockSpec((depth, columns), lambda i: (0, 0)),
            pl.BlockSpec((tile, depth), lambda i: (i, 0)),
        ],
        out_specs=[pl.BlockSpec((groups * block, tile), lambda i: (0, i))] * parts,
        out_shape=[jax.ShapeDtypeStruct((groups * block, rows), jnp.float32)] * parts,
        scratch_shapes=[pltpu.VMEM((columns, depth), jnp.bfloat16)],
        compiler_params=pltpu.CompilerParams(vmem_limit_bytes=48 * MIB),
        cost_estimate=pl.CostEstimate(
            flops=2 * rows * depth * columns, bytes_accessed=2 * rows * depth, transcendentals=0
        ),
    )(lwe, database)


def at_end():
    z = lax.axis_index("col")
    return jnp.logical_or(z == 0, z == 3)


def role_block(role):
    place = jnp.where(at_end(), role[0], role[1])
    return jnp.where(lax.axis_index("col") >= 2, place, 3 - place)


def line_hint_kernel(roles, cuts, tile, lwe_ref, data_ref, *rest):
    outs = rest[: sum(len(c) for c in cuts)]
    lwe_v, data_v, turned, lwe_sem, data_sem = rest[len(outs) :]
    rows = data_ref.shape[0]
    own = lwe_v.shape[2]
    copies = []
    for b, role in enumerate(roles):
        at = pl.multiple_of(role_block(role) * own, own)
        copies.append(pltpu.make_async_copy(lwe_ref.at[:, pl.ds(at, own)], lwe_v.at[b], lwe_sem.at[b]))
    tiles = []
    for i in range(rows // tile):
        at = slice(i * tile, (i + 1) * tile)
        tiles.append(pltpu.make_async_copy(data_ref.at[at, :], data_v.at[at, :], data_sem.at[i]))
    for c in copies + tiles:
        c.start()
    for b, c in enumerate(copies):
        c.wait()
        turned[b * own : (b + 1) * own, :] = lwe_v[b].T
    for i, c in enumerate(tiles):
        c.wait()
        at = slice(i * tile, (i + 1) * tile)
        res = lax.dot_general(
            turned[...], data_v[at, :], (((1,), (1,)), ((), ())), preferred_element_type=jnp.float32
        )
        n = 0
        for b in range(len(roles)):
            top = b * own
            for rows_k in cuts[b]:
                outs[n][:, at] = res[top : top + rows_k, :]
                top += rows_k
                n += 1


def line_hint(lwe, database, roles, cuts):
    depth, columns = lwe.shape
    rows = database.shape[0]
    own = columns // 4
    tile = min(512, rows)
    flat = pl.pallas_call(
        functools.partial(line_hint_kernel, roles, cuts, tile),
        in_specs=[pl.BlockSpec(memory_space=pl.ANY)] * 2,
        out_shape=[jax.ShapeDtypeStruct((k, rows), jnp.float32) for c in cuts for k in c],
        scratch_shapes=[
            pltpu.VMEM((len(roles), depth, own), jnp.bfloat16),
            pltpu.VMEM((rows, depth), jnp.bfloat16),
            pltpu.VMEM((len(roles) * own, depth), jnp.bfloat16),
            pltpu.SemaphoreType.DMA((len(roles),)),
            pltpu.SemaphoreType.DMA((rows // tile,)),
        ],
        compiler_params=pltpu.CompilerParams(vmem_limit_bytes=56 * MIB),
        cost_estimate=pl.CostEstimate(
            flops=2 * rows * depth * own * len(roles), bytes_accessed=2 * rows * depth, transcendentals=0
        ),
    )(lwe, database)
    out, n = [], 0
    for c in cuts:
        out.append(list(flat[n : n + len(c)]))
        n += len(c)
    return out


def pass_kernel(cuts, own_ref, got_ref, *outs):
    top = 0
    keep = jnp.where(at_end(), 0.0, 1.0)
    for k, rows in enumerate(cuts):
        at = slice(top, top + rows)
        outs[k][...] = own_ref[at, :] + got_ref[at, :] * keep
        top += rows


def pass_on(own, got, cuts):
    return pl.pallas_call(
        functools.partial(pass_kernel, cuts),
        out_shape=[jax.ShapeDtypeStruct((k, own.shape[1]), jnp.float32) for k in cuts],
        compiler_params=pltpu.CompilerParams(vmem_limit_bytes=16 * MIB),
        cost_estimate=pl.CostEstimate(flops=own.size, bytes_accessed=0, transcendentals=0),
    )(own, got)


def final_kernel(own_ref, near_ref, direct_ref, cross_ref, last_ref, sum_ref):
    keep = jnp.where(at_end(), 1.0, 0.0)
    sum_ref[...] = (own_ref[...] + near_ref[...] * keep) + (direct_ref[...] + cross_ref[...]) + last_ref[...]


def final_hint(top, own, near, direct, cross, last):
    cut = pl.BlockSpec(last.shape, lambda i: (top // last.shape[0], 0))
    whole = pl.BlockSpec(last.shape, lambda i: (0, 0))
    return pl.pallas_call(
        final_kernel,
        grid=(1,),
        in_specs=[cut, cut, cut, cut, whole],
        out_specs=whole,
        out_shape=jax.ShapeDtypeStruct(last.shape, jnp.float32),
        compiler_params=pltpu.CompilerParams(vmem_limit_bytes=16 * MIB),
        cost_estimate=pl.CostEstimate(flops=last.size, bytes_accessed=0, transcendentals=0),
    )(own, near, direct, cross, last)


def swap_kernel(radix, in_ref, out_ref, stage):
    groups, rows = in_ref.shape[:2]
    for k in range(radix):
        lanes = slice(k * LANES, (k + 1) * LANES)
        stage[lanes, :] = in_ref[:, :, lanes].reshape(groups * rows, LANES).T
    for r in range(radix):
        picked = stage[pl.ds(r, LANES, stride=radix), :].T
        out_ref[:, :, r * LANES : (r + 1) * LANES] = picked.reshape(groups, rows, LANES)


def swap_digits(cipher, offset, rows):
    points = cipher.shape[2]
    radix = points // LANES
    return pl.pallas_call(
        functools.partial(swap_kernel, radix),
        grid=(1,),
        in_specs=[pl.BlockSpec((4, rows, points), lambda i: (0, offset // rows, 0))],
        out_specs=pl.BlockSpec((4, rows, points), lambda i: (0, 0, 0)),
        out_shape=jax.ShapeDtypeStruct((4, rows, points), jnp.float32),
        scratch_shapes=[pltpu.VMEM((points, 4 * rows), jnp.float32)],
        compiler_params=pltpu.CompilerParams(vmem_limit_bytes=16 * MIB),
        cost_estimate=pl.CostEstimate(flops=0, bytes_accessed=32 * rows * points, transcendentals=0),
    )(cipher)


def fft_list(re, im):
    n = len(re)
    if n == 1:
        return re, im
    er, ei = fft_list(re[0::2], im[0::2])
    odd_r, odd_i = fft_list(re[1::2], im[1::2])
    half = n // 2
    out_r, out_i = [None] * n, [None] * n
    for k in range(half):
        xr, xi = odd_r[k], odd_i[k]
        if k == 0:
            tr, ti = xr, xi
        elif 4 * k == n:
            tr, ti = xi, -xr
        elif 8 * k == n:
            c = math.sqrt(0.5)
            tr, ti = (xr + xi) * c, (xi - xr) * c
        elif 8 * k == 3 * n:
            c = math.sqrt(0.5)
            tr, ti = (xi - xr) * c, -(xr + xi) * c
        else:
            c, s = math.cos(2 * math.pi * k / n), math.sin(2 * math.pi * k / n)
            tr, ti = xr * c + xi * s, xi * c - xr * s
        out_r[k], out_i[k] = er[k] + tr, ei[k] + ti
        out_r[k + half], out_i[k + half] = er[k] - tr, ei[k] - ti
    return out_r, out_i


def transform_kernel(blocks, radix, rows, *refs):
    hints = refs[:blocks]
    first_ref, twist_ref, table_hi, table_lo, cipher_ref, total_ref, out_ref, stage = refs[blocks:]
    for top in range(0, rows, 8):
        re, im = [], []
        for u in range(radix):
            lanes = slice(u * LANES, (u + 1) * LANES)
            real = imag = None
            for b in range(blocks):
                h = hints[b][top : top + 8, lanes]
                x, y = h * first_ref[2 * b : 2 * b + 1, lanes], h * first_ref[2 * b + 1 : 2 * b + 2, lanes]
                real = x if real is None else real + x
                imag = y if imag is None else imag + y
            re.append(real)
            im.append(imag)
        re, im = fft_list(re, im)
        for r in range(radix):
            c = twist_ref[2 * r : 2 * r + 1, :]
            s = twist_ref[2 * r + 1 : 2 * r + 2, :]
            at = slice(r * rows + top, r * rows + top + 8)
            stage[at, :LANES] = re[r] * c + im[r] * s
            stage[at, LANES:] = im[r] * c - re[r] * s
    for r in range(radix):
        high, low = split_bf16(stage[r * rows : (r + 1) * rows, :])
        dot = functools.partial(jnp.dot, preferred_element_type=jnp.float32)
        spec = dot(high, table_hi[...]) + (dot(low, table_hi[...]) + dot(high, table_lo[...]))
        sr, si = spec[:, :LANES], spec[:, LANES:]
        lanes = slice(r * LANES, (r + 1) * LANES)
        for c in range(2):
            a, b = cipher_ref[2 * c, :, lanes], cipher_ref[2 * c + 1, :, lanes]
            real = jnp.sum(sr * a - si * b, axis=0, keepdims=True)
            imag = jnp.sum(sr * b + si * a, axis=0, keepdims=True)
            out_ref[2 * c : 2 * c + 1, lanes] = total_ref[2 * c : 2 * c + 1, lanes] + real
            out_ref[2 * c + 1 : 2 * c + 2, lanes] = total_ref[2 * c + 1 : 2 * c + 2, lanes] + imag


def transform_products(hints, first, twist, tables, cipher, part, total):
    rows, points = hints[0].shape
    radix = points // LANES
    whole = lambda a: pl.BlockSpec(a.shape, lambda i: (0,) * a.ndim)
    return pl.pallas_call(
        functools.partial(transform_kernel, len(hints), radix, rows),
        grid=(1,),
        in_specs=[whole(h) for h in hints]
        + [whole(first), whole(twist), whole(tables[0]), whole(tables[1])]
        + [pl.BlockSpec((4, rows, points), lambda i: (0, part, 0)), whole(total)],
        out_specs=pl.BlockSpec((4, points), lambda i: (0, 0)),
        out_shape=jax.ShapeDtypeStruct((4, points), jnp.float32),
        scratch_shapes=[pltpu.VMEM((radix * rows, 2 * LANES), jnp.float32)],
        compiler_params=pltpu.CompilerParams(vmem_limit_bytes=32 * MIB),
        cost_estimate=pl.CostEstimate(
            flops=6 * radix * rows * 256 * 256, bytes_accessed=24 * rows * points, transcendentals=0
        ),
    )(*hints, first, twist, *tables, cipher, total)


def xor_pairs(size, step):
    return [(i, i ^ step) for i in range(size)]


def sum_over(x, axes):
    for axis in axes:
        size = lax.axis_size(axis)
        if size & (size - 1):
            x = lax.psum(x, axis)
            continue
        step = 1
        while step < size:
            x = x + lax.ppermute(x, axis, xor_pairs(size, step))
            step *= 2
    return x


def line_parts(lwe, database, cipher, cuts):
    own = cipher.shape[1]
    (first,), (far_mid,), (kept,), (later,) = line_hint(
        lwe, database, [(0, 3), (1, 1), (3, 2), (2, 0)], [[own]] * 4
    )
    near = lax.ppermute(first, "col", NEIGHBOURS)
    direct = lax.ppermute(far_mid, "col", END_TO_FAR_MIDDLE)
    cross = lax.ppermute(far_mid, "col", CROSS)
    cipher = lax.optimization_barrier((cipher, first))[0]
    tops = [sum(cuts[:k]) for k in range(len(cuts))]
    swapped = [swap_digits(cipher, top, rows) for top, rows in zip(tops, cuts)]
    near, swapped = lax.optimization_barrier((near, swapped))
    last = [lax.ppermute(x, "col", ROUND) for x in pass_on(later, near, cuts)]
    for k, top in enumerate(tops):
        mine = final_hint(top, kept, near, direct, cross, last[k])
        yield [mine, lax.ppermute(mine, "row", SWAP)], swapped[k]


def body(parts, database, lwe_matrix, secret_ct):
    row_count, row_rank = lax.axis_size("row"), lax.axis_index("row")
    col_count = lax.axis_size("col")
    points = database.shape[0]
    degree = points * row_count
    radix = points // LANES
    own = secret_ct.shape[3]

    source = (row_rank + jnp.arange(row_count, dtype=jnp.int32)) % row_count if row_count == 2 else jnp.arange(row_count, dtype=jnp.int32)
    index = (source[:, None] * points + jnp.arange(points, dtype=jnp.int32)[None, :]) * (2 * row_rank + 1) % (2 * degree)
    angle = index.astype(jnp.float32) * (np.pi / degree)
    first = jnp.stack([jnp.cos(angle), -jnp.sin(angle)], axis=1).reshape(2 * row_count, points)
    lane = np.arange(LANES)
    turn = 2 * np.pi * (np.arange(radix)[:, None] * lane[None, :] % points) / points
    twist = jnp.asarray(np.stack([np.cos(turn), np.sin(turn)], axis=1).reshape(2 * radix, LANES), jnp.float32)
    small = 2 * np.pi * (lane[:, None] * lane[None, :] % LANES) / LANES
    table = np.block([[np.cos(small), -np.sin(small)], [np.sin(small), np.cos(small)]]).astype(np.float32)
    high = table.astype(jnp.bfloat16)
    low = (table - high.astype(np.float32)).astype(jnp.bfloat16)
    tables = (jnp.asarray(high), jnp.asarray(low))

    lwe = lwe_matrix[:, 0, :]
    cipher = secret_ct.reshape(4, own, points)
    total = jnp.zeros((4, points), jnp.float32)
    if col_count == 4 and row_count == 2 and own == LANES and points % 512 == 0:
        cuts = [32, 32, 32, 32]
        for hints, swapped in line_parts(lwe, database, cipher, cuts):
            total = transform_products(hints, first, twist, tables, swapped, 0, total)
    else:
        swapped = cipher.reshape(4, own, LANES, radix).swapaxes(2, 3).reshape(4, own, points)
        partial = partial_hint(lwe, database, col_count, parts)
        for k in range(parts):
            mine = lax.psum_scatter(partial[k], "col", scatter_dimension=0, tiled=True)
            if row_count == 2:
                hints = [mine, lax.ppermute(mine, "row", SWAP)]
            else:
                gathered = lax.all_gather(mine, "row")
                hints = [gathered[b] for b in range(row_count)]
            total = transform_products(hints, first, twist, tables, swapped, k, total)
    total = sum_over(total, ("limb", "col"))
    scale = 1.0 / (math.sqrt(degree) * math.sqrt(2 * lwe_matrix.shape[2]))
    total = total.reshape(4, radix, LANES).swapaxes(1, 2).reshape(2, 2, points)
    return total * scale


def solution(mesh):
    placed = (P(("grp", "row"), "col"), P("col", "limb", None), P(None, None, "limb", "col", "row"))

    def whole(database, lwe_matrix, secret_ct):
        own = lwe_matrix.shape[2] // mesh.shape["col"]
        parts = 2 if own % 16 == 0 else 1
        return jax.shard_map(
            functools.partial(body, parts), mesh=mesh, in_specs=placed, out_specs=P("grp", None, "row"), check_vma=False
        )(database, lwe_matrix, secret_ct)

    return whole
```

```python
import functools
import math

import jax
import jax.numpy as jnp
import numpy as np
from jax import lax
from jax.experimental import pallas as pl
from jax.experimental.pallas import tpu as pltpu
from jax.sharding import PartitionSpec as P

LANES = 128
MIB = 1 << 20
SWAP = [(0, 1), (1, 0)]
NEIGHBOURS = [(0, 1), (1, 0), (2, 3), (3, 2)]
END_TO_FAR_MIDDLE = [(0, 2), (3, 1)]
CROSS = [(1, 2), (2, 1)]
ROUND = [(0, 1), (1, 3), (3, 2), (2, 0)]


def split_bf16(x):
    high = x.astype(jnp.bfloat16)
    low = (x - high.astype(jnp.float32)).astype(jnp.bfloat16)
    return high, low


def hint_kernel(groups, parts, block, lwe_ref, data_ref, *rest):
    outs, turned = rest[:-1], rest[-1]

    @pl.when(pl.program_id(0) == 0)
    def _():
        turned[...] = lwe_ref[...].T

    for g in range(groups):
        rows = slice(g * parts * block, (g + 1) * parts * block)
        res = lax.dot_general(
            turned[rows, :], data_ref[...], (((1,), (1,)), ((), ())), preferred_element_type=jnp.float32
        )
        for k in range(parts):
            outs[k][g * block : (g + 1) * block, :] = res[k * block : (k + 1) * block, :]


def partial_hint(lwe, database, groups, parts):
    depth, columns = lwe.shape
    rows = database.shape[0]
    block = columns // (groups * parts)
    tile = min(256, rows)
    return pl.pallas_call(
        functools.partial(hint_kernel, groups, parts, block),
        grid=(rows // tile,),
        in_specs=[
            pl.BlockSpec((depth, columns), lambda i: (0, 0)),
            pl.BlockSpec((tile, depth), lambda i: (i, 0)),
        ],
        out_specs=[pl.BlockSpec((groups * block, tile), lambda i: (0, i))] * parts,
        out_shape=[jax.ShapeDtypeStruct((groups * block, rows), jnp.float32)] * parts,
        scratch_shapes=[pltpu.VMEM((columns, depth), jnp.bfloat16)],
        compiler_params=pltpu.CompilerParams(vmem_limit_bytes=48 * MIB),
        cost_estimate=pl.CostEstimate(
            flops=2 * rows * depth * columns, bytes_accessed=2 * rows * depth, transcendentals=0
        ),
    )(lwe, database)


def at_end():
    z = lax.axis_index("col")
    return jnp.logical_or(z == 0, z == 3)


def role_block(role):
    place = jnp.where(at_end(), role[0], role[1])
    return jnp.where(lax.axis_index("col") >= 2, place, 3 - place)


def line_hint_kernel(roles, cuts, tile, lwe_ref, data_ref, *rest):
    outs = rest[: sum(len(c) for c in cuts)]
    lwe_v, data_v, turned, lwe_sem, data_sem = rest[len(outs) :]
    rows = data_ref.shape[0]
    own = lwe_v.shape[2]
    copies = []
    for b, role in enumerate(roles):
        at = pl.multiple_of(role_block(role) * own, own)
        copies.append(pltpu.make_async_copy(lwe_ref.at[:, pl.ds(at, own)], lwe_v.at[b], lwe_sem.at[b]))
    tiles = []
    for i in range(rows // tile):
        at = slice(i * tile, (i + 1) * tile)
        tiles.append(pltpu.make_async_copy(data_ref.at[at, :], data_v.at[at, :], data_sem.at[i]))
    for c in copies + tiles:
        c.start()
    for b, c in enumerate(copies):
        c.wait()
        turned[b * own : (b + 1) * own, :] = lwe_v[b].T
    for i, c in enumerate(tiles):
        c.wait()
        at = slice(i * tile, (i + 1) * tile)
        res = lax.dot_general(
            turned[...], data_v[at, :], (((1,), (1,)), ((), ())), preferred_element_type=jnp.float32
        )
        n = 0
        for b in range(len(roles)):
            top = b * own
            for rows_k in cuts[b]:
                outs[n][:, at] = res[top : top + rows_k, :]
                top += rows_k
                n += 1


def line_hint(lwe, database, roles, cuts):
    depth, columns = lwe.shape
    rows = database.shape[0]
    own = columns // 4
    tile = min(512, rows)
    flat = pl.pallas_call(
        functools.partial(line_hint_kernel, roles, cuts, tile),
        in_specs=[pl.BlockSpec(memory_space=pl.ANY)] * 2,
        out_shape=[jax.ShapeDtypeStruct((k, rows), jnp.float32) for c in cuts for k in c],
        scratch_shapes=[
            pltpu.VMEM((len(roles), depth, own), jnp.bfloat16),
            pltpu.VMEM((rows, depth), jnp.bfloat16),
            pltpu.VMEM((len(roles) * own, depth), jnp.bfloat16),
            pltpu.SemaphoreType.DMA((len(roles),)),
            pltpu.SemaphoreType.DMA((rows // tile,)),
        ],
        compiler_params=pltpu.CompilerParams(vmem_limit_bytes=56 * MIB),
        cost_estimate=pl.CostEstimate(
            flops=2 * rows * depth * own * len(roles), bytes_accessed=2 * rows * depth, transcendentals=0
        ),
    )(lwe, database)
    out, n = [], 0
    for c in cuts:
        out.append(list(flat[n : n + len(c)]))
        n += len(c)
    return out


def swap_kernel(radix, in_ref, out_ref, stage):
    groups, rows = in_ref.shape[:2]
    some = stage.shape[2] // rows
    for n in range(groups // some):
        at = slice(n * some, (n + 1) * some)
        for k in range(radix):
            lanes = slice(k * LANES, (k + 1) * LANES)
            stage[n, lanes, :] = in_ref[at, :, lanes].reshape(some * rows, LANES).T
        for r in range(radix):
            picked = stage[n, pl.ds(r, LANES, stride=radix), :].T
            out_ref[at, :, r * LANES : (r + 1) * LANES] = picked.reshape(some, rows, LANES)


def swap_digits(cipher, offset, rows):
    points = cipher.shape[2]
    radix = points // LANES
    return pl.pallas_call(
        functools.partial(swap_kernel, radix),
        grid=(1,),
        in_specs=[pl.BlockSpec((4, rows, points), lambda i: (0, offset // rows, 0))],
        out_specs=pl.BlockSpec((4, rows, points), lambda i: (0, 0, 0)),
        out_shape=jax.ShapeDtypeStruct((4, rows, points), jnp.float32),
        scratch_shapes=[pltpu.VMEM((max(1, 4 * rows // LANES), points, min(4 * rows, LANES)), jnp.float32)],
        compiler_params=pltpu.CompilerParams(vmem_limit_bytes=16 * MIB),
        cost_estimate=pl.CostEstimate(flops=0, bytes_accessed=32 * rows * points, transcendentals=0),
    )(cipher)


def fft_list(re, im):
    n = len(re)
    if n == 1:
        return re, im
    er, ei = fft_list(re[0::2], im[0::2])
    odd_r, odd_i = fft_list(re[1::2], im[1::2])
    half = n // 2
    out_r, out_i = [None] * n, [None] * n
    for k in range(half):
        xr, xi = odd_r[k], odd_i[k]
        if k == 0:
            tr, ti = xr, xi
        elif 4 * k == n:
            tr, ti = xi, -xr
        elif 8 * k == n:
            c = math.sqrt(0.5)
            tr, ti = (xr + xi) * c, (xi - xr) * c
        elif 8 * k == 3 * n:
            c = math.sqrt(0.5)
            tr, ti = (xi - xr) * c, -(xr + xi) * c
        else:
            c, s = math.cos(2 * math.pi * k / n), math.sin(2 * math.pi * k / n)
            tr, ti = xr * c + xi * s, xi * c - xr * s
        out_r[k], out_i[k] = er[k] + tr, ei[k] + ti
        out_r[k + half], out_i[k + half] = er[k] - tr, ei[k] - ti
    return out_r, out_i


def transform_kernel(blocks, radix, rows, *refs):
    hints = refs[:blocks]
    first_ref, twist_ref, table_hi, table_lo, cipher_ref, total_ref, out_ref, stage = refs[blocks:]
    for top in range(0, rows, 8):
        re, im = [], []
        for u in range(radix):
            lanes = slice(u * LANES, (u + 1) * LANES)
            real = imag = None
            for b in range(blocks):
                h = hints[b][top : top + 8, lanes]
                x, y = h * first_ref[2 * b : 2 * b + 1, lanes], h * first_ref[2 * b + 1 : 2 * b + 2, lanes]
                real = x if real is None else real + x
                imag = y if imag is None else imag + y
            re.append(real)
            im.append(imag)
        re, im = fft_list(re, im)
        for r in range(radix):
            c = twist_ref[2 * r : 2 * r + 1, :]
            s = twist_ref[2 * r + 1 : 2 * r + 2, :]
            at = slice(r * rows + top, r * rows + top + 8)
            stage[at, :LANES] = re[r] * c + im[r] * s
            stage[at, LANES:] = im[r] * c - re[r] * s
    for r in range(radix):
        high, low = split_bf16(stage[r * rows : (r + 1) * rows, :])
        dot = functools.partial(jnp.dot, preferred_element_type=jnp.float32)
        spec = dot(high, table_hi[...]) + (dot(low, table_hi[...]) + dot(high, table_lo[...]))
        sr, si = spec[:, :LANES], spec[:, LANES:]
        lanes = slice(r * LANES, (r + 1) * LANES)
        for c in range(2):
            a, b = cipher_ref[2 * c, :, lanes], cipher_ref[2 * c + 1, :, lanes]
            real = jnp.sum(sr * a - si * b, axis=0, keepdims=True)
            imag = jnp.sum(sr * b + si * a, axis=0, keepdims=True)
            out_ref[2 * c : 2 * c + 1, lanes] = total_ref[2 * c : 2 * c + 1, lanes] + real
            out_ref[2 * c + 1 : 2 * c + 2, lanes] = total_ref[2 * c + 1 : 2 * c + 2, lanes] + imag


def transform_products(hints, tables, cipher, total):
    rows, points = hints[0].shape
    radix = points // LANES
    return pl.pallas_call(
        functools.partial(transform_kernel, len(hints), radix, rows),
        out_shape=jax.ShapeDtypeStruct((4, points), jnp.float32),
        scratch_shapes=[pltpu.VMEM((radix * rows, 2 * LANES), jnp.float32)],
        compiler_params=pltpu.CompilerParams(vmem_limit_bytes=16 * MIB),
        cost_estimate=pl.CostEstimate(
            flops=6 * radix * rows * 256 * 256, bytes_accessed=0, transcendentals=0
        ),
    )(*hints, *tables, cipher, total)


def xor_pairs(size, step):
    return [(i, i ^ step) for i in range(size)]


def sum_over(x, axis):
    size = lax.axis_size(axis)
    if size == 4:
        near, far, across = [lax.ppermute(x, axis, xor_pairs(size, step)) for step in (1, 2, 3)]
        return (x + near) + (far + across)
    if size & (size - 1):
        return lax.psum(x, axis)
    step = 1
    while step < size:
        x = x + lax.ppermute(x, axis, xor_pairs(size, step))
        step *= 2
    return x


def line_total(lwe, database, cipher, tables, total, cuts):
    own = cipher.shape[1]
    tops = [sum(cuts[:k]) for k in range(len(cuts))]
    ats = [slice(top, top + rows) for top, rows in zip(tops, cuts)]
    (first,), far_mid = line_hint(lwe, database, [(0, 3), (1, 1)], [[own], cuts])
    near = lax.ppermute(first, "col", NEIGHBOURS)
    cross = [lax.ppermute(jnp.concatenate(far_mid, axis=0), "col", CROSS)]
    direct = [lax.ppermute(far_mid[0], "col", END_TO_FAR_MIDDLE)]
    lwe, database, cipher = lax.optimization_barrier((lwe, database, cipher, first))[:3]
    (kept,), (later,) = line_hint(lwe, database, [(3, 2), (2, 0)], [[own]] * 2)
    swapped = [swap_digits(cipher, top, rows) for top, rows in zip(tops, cuts)]
    near, kept, swapped, far_mid = lax.optimization_barrier((near, kept, swapped, far_mid))
    end = at_end()
    passed = later + jnp.where(end, 0.0, near)
    last = [lax.ppermute(passed[at], "col", ROUND) for at in ats]
    direct += [lax.ppermute(x, "col", END_TO_FAR_MIDDLE) for x in far_mid[1:]]
    sums, mine = [total], None
    for k, at in enumerate(ats):
        got = last[k]
        if k >= 2:
            got, sums[k - 1] = lax.optimization_barrier((got, sums[k - 1]))
        if k >= 1:
            got, mine = lax.optimization_barrier((got, mine))
        mine = (kept[at] + jnp.where(end, near[at], 0.0)) + (cross[0][at] + direct[k]) + got
        sums.append(transform_products([mine, lax.ppermute(mine, "row", SWAP)], tables, swapped[k], sums[k]))
    return sums[-1]


def body(parts, database, lwe_matrix, secret_ct):
    row_count, row_rank = lax.axis_size("row"), lax.axis_index("row")
    col_count = lax.axis_size("col")
    points = database.shape[0]
    degree = points * row_count
    radix = points // LANES
    own = secret_ct.shape[3]

    source = (row_rank + jnp.arange(row_count, dtype=jnp.int32)) % row_count if row_count == 2 else jnp.arange(row_count, dtype=jnp.int32)
    index = (source[:, None] * points + jnp.arange(points, dtype=jnp.int32)[None, :]) * (2 * row_rank + 1) % (2 * degree)
    angle = index.astype(jnp.float32) * (np.pi / degree)
    first = jnp.stack([jnp.cos(angle), -jnp.sin(angle)], axis=1).reshape(2 * row_count, points)
    lane = np.arange(LANES)
    turn = 2 * np.pi * (np.arange(radix)[:, None] * lane[None, :] % points) / points
    twist = jnp.asarray(np.stack([np.cos(turn), np.sin(turn)], axis=1).reshape(2 * radix, LANES), jnp.float32)
    small = 2 * np.pi * (lane[:, None] * lane[None, :] % LANES) / LANES
    table = np.block([[np.cos(small), -np.sin(small)], [np.sin(small), np.cos(small)]]).astype(np.float32)
    high = table.astype(jnp.bfloat16)
    low = (table - high.astype(np.float32)).astype(jnp.bfloat16)
    tables = (first, twist, jnp.asarray(high), jnp.asarray(low))

    lwe = lwe_matrix[:, 0, :]
    cipher = secret_ct.reshape(4, own, points)
    total = jnp.zeros((4, points), jnp.float32)
    if col_count == 4 and row_count == 2 and own == LANES and points % 512 == 0:
        cuts = [64, 32, 32]
        total = line_total(lwe, database, cipher, tables, total, cuts)
    else:
        swapped = cipher.reshape(4, own, LANES, radix).swapaxes(2, 3).reshape(4, own, points)
        partial = partial_hint(lwe, database, col_count, parts)
        block = own // parts
        for k in range(parts):
            mine = lax.psum_scatter(partial[k], "col", scatter_dimension=0, tiled=True)
            if row_count == 2:
                hints = [mine, lax.ppermute(mine, "row", SWAP)]
            else:
                gathered = lax.all_gather(mine, "row")
                hints = [gathered[b] for b in range(row_count)]
            total = transform_products(hints, tables, swapped[:, k * block : (k + 1) * block], total)
    total = sum_over(sum_over(total, "limb"), "col")
    scale = 1.0 / (math.sqrt(degree) * math.sqrt(2 * lwe_matrix.shape[2]))
    total = total.reshape(4, radix, LANES).swapaxes(1, 2).reshape(2, 2, points)
    return total * scale


def solution(mesh):
    placed = (P(("grp", "row"), "col"), P("col", "limb", None), P(None, None, "limb", "col", "row"))

    def whole(database, lwe_matrix, secret_ct):
        own = lwe_matrix.shape[2] // mesh.shape["col"]
        parts = 2 if own % 16 == 0 else 1
        return jax.shard_map(
            functools.partial(body, parts), mesh=mesh, in_specs=placed, out_specs=P("grp", None, "row"), check_vma=False
        )(database, lwe_matrix, secret_ct)

    return whole
```

```python
import functools
import math

import jax
import jax.numpy as jnp
import numpy as np
from jax import lax
from jax.experimental import pallas as pl
from jax.experimental.pallas import tpu as pltpu
from jax.sharding import PartitionSpec as P

LANES = 128
MIB = 1 << 20
SWAP = [(0, 1), (1, 0)]
INWARD = [(0, 1), (3, 2)]
NEIGHBOURS = [(0, 1), (1, 0), (2, 3), (3, 2)]
END_TO_FAR_MIDDLE = [(0, 2), (3, 1)]
CROSS = [(1, 2), (2, 1)]
ROUND = [(0, 1), (1, 3), (3, 2), (2, 0)]


def split_bf16(x):
    high = x.astype(jnp.bfloat16)
    low = (x - high.astype(jnp.float32)).astype(jnp.bfloat16)
    return high, low


def hint_kernel(groups, parts, block, lwe_ref, data_ref, *rest):
    outs, turned = rest[:-1], rest[-1]

    @pl.when(pl.program_id(0) == 0)
    def _():
        turned[...] = lwe_ref[...].T

    for g in range(groups):
        rows = slice(g * parts * block, (g + 1) * parts * block)
        res = lax.dot_general(
            turned[rows, :], data_ref[...], (((1,), (1,)), ((), ())), preferred_element_type=jnp.float32
        )
        for k in range(parts):
            outs[k][g * block : (g + 1) * block, :] = res[k * block : (k + 1) * block, :]


def partial_hint(lwe, database, groups, parts):
    depth, columns = lwe.shape
    rows = database.shape[0]
    block = columns // (groups * parts)
    tile = min(256, rows)
    return pl.pallas_call(
        functools.partial(hint_kernel, groups, parts, block),
        grid=(rows // tile,),
        in_specs=[
            pl.BlockSpec((depth, columns), lambda i: (0, 0)),
            pl.BlockSpec((tile, depth), lambda i: (i, 0)),
        ],
        out_specs=[pl.BlockSpec((groups * block, tile), lambda i: (0, i))] * parts,
        out_shape=[jax.ShapeDtypeStruct((groups * block, rows), jnp.float32)] * parts,
        scratch_shapes=[pltpu.VMEM((columns, depth), jnp.bfloat16)],
        compiler_params=pltpu.CompilerParams(vmem_limit_bytes=48 * MIB),
        cost_estimate=pl.CostEstimate(
            flops=2 * rows * depth * columns, bytes_accessed=2 * rows * depth, transcendentals=0
        ),
    )(lwe, database)


def at_end():
    z = lax.axis_index("col")
    return jnp.logical_or(z == 0, z == 3)


def role_block(role):
    place = jnp.where(at_end(), role[0], role[1])
    return jnp.where(lax.axis_index("col") >= 2, place, 3 - place)


def line_hint_kernel(roles, cuts, tile, lwe_ref, data_ref, *rest):
    pieces = [(b, top, size) for b, c in enumerate(cuts) for top, size in c]
    outs = rest[: len(pieces)]
    lwe_v, data_v, turned, made, lwe_sem, data_sem, out_sem = rest[len(pieces) :]
    rows = data_ref.shape[0]
    own = made.shape[0] // len(roles)
    lwe_copy = pltpu.make_async_copy(lwe_ref, lwe_v, lwe_sem)
    lwe_copy.start()
    tiles = []
    for i in range(rows // tile):
        at = slice(i * tile, (i + 1) * tile)
        tiles.append(pltpu.make_async_copy(data_ref.at[at, :], data_v.at[at, :], data_sem.at[i]))
        tiles[-1].start()
    lwe_copy.wait()
    for b, role in enumerate(roles):
        at = pl.multiple_of(role_block(role) * own, own)
        turned[b * own : (b + 1) * own, :] = lwe_v[:, pl.ds(at, own)].T
    written = []
    for i, c in enumerate(tiles):
        c.wait()
        at = slice(i * tile, (i + 1) * tile)
        made[:, at] = lax.dot_general(
            turned[...], data_v[at, :], (((1,), (1,)), ((), ())), preferred_element_type=jnp.float32
        )
        for n, (b, top, size) in enumerate(pieces):
            source = made.at[b * own + top : b * own + top + size, at]
            written.append(pltpu.make_async_copy(source, outs[n].at[:, at], out_sem.at[i * len(pieces) + n]))
            written[-1].start()
    for c in written:
        c.wait()


def line_hint(lwe, database, roles, cuts, limit):
    depth, columns = lwe.shape
    rows = database.shape[0]
    own = columns // 4
    tile = min(512, rows)
    flat = pl.pallas_call(
        functools.partial(line_hint_kernel, roles, cuts, tile),
        in_specs=[pl.BlockSpec(memory_space=pl.ANY)] * 2,
        out_shape=[jax.ShapeDtypeStruct((k, rows), jnp.float32) for c in cuts for _, k in c],
        out_specs=[pl.BlockSpec(memory_space=pl.ANY)] * sum(len(c) for c in cuts),
        scratch_shapes=[
            pltpu.VMEM((depth, columns), jnp.bfloat16),
            pltpu.VMEM((rows, depth), jnp.bfloat16),
            pltpu.VMEM((len(roles) * own, depth), jnp.bfloat16),
            pltpu.VMEM((len(roles) * own, rows), jnp.float32),
            pltpu.SemaphoreType.DMA,
            pltpu.SemaphoreType.DMA((rows // tile,)),
            pltpu.SemaphoreType.DMA((rows // tile * sum(len(c) for c in cuts),)),
        ],
        compiler_params=pltpu.CompilerParams(vmem_limit_bytes=limit * MIB),
        cost_estimate=pl.CostEstimate(
            flops=2 * rows * depth * own * len(roles), bytes_accessed=2 * rows * depth, transcendentals=0
        ),
    )(lwe, database)
    out, n = [], 0
    for c in cuts:
        out.append(list(flat[n : n + len(c)]))
        n += len(c)
    return out


def swap_kernel(radix, in_ref, out_ref, stage):
    groups, rows = in_ref.shape[:2]
    some = stage.shape[2] // groups
    for n in range(rows // some):
        at = slice(n * some, (n + 1) * some)
        for k in range(radix):
            lanes = slice(k * LANES, (k + 1) * LANES)
            stage[n, lanes, :] = in_ref[:, at, lanes].reshape(groups * some, LANES).T
        for r in range(radix):
            picked = stage[n, pl.ds(r, LANES, stride=radix), :].T
            out_ref[:, at, r * LANES : (r + 1) * LANES] = picked.reshape(groups, some, LANES)


def swap_digits(cipher, offset, rows):
    points = cipher.shape[2]
    radix = points // LANES
    return pl.pallas_call(
        functools.partial(swap_kernel, radix),
        grid=(1,),
        in_specs=[pl.BlockSpec((4, rows, points), lambda i: (0, offset // rows, 0))],
        out_specs=pl.BlockSpec((4, rows, points), lambda i: (0, 0, 0)),
        out_shape=jax.ShapeDtypeStruct((4, rows, points), jnp.float32),
        scratch_shapes=[pltpu.VMEM((max(1, rows // 32), points, min(4 * rows, LANES)), jnp.float32)],
        compiler_params=pltpu.CompilerParams(vmem_limit_bytes=16 * MIB),
        cost_estimate=pl.CostEstimate(flops=0, bytes_accessed=32 * rows * points, transcendentals=0),
    )(cipher)


def fft_list(re, im):
    n = len(re)
    if n == 1:
        return re, im
    er, ei = fft_list(re[0::2], im[0::2])
    odd_r, odd_i = fft_list(re[1::2], im[1::2])
    half = n // 2
    out_r, out_i = [None] * n, [None] * n
    for k in range(half):
        xr, xi = odd_r[k], odd_i[k]
        if k == 0:
            tr, ti = xr, xi
        elif 4 * k == n:
            tr, ti = xi, -xr
        elif 8 * k == n:
            c = math.sqrt(0.5)
            tr, ti = (xr + xi) * c, (xi - xr) * c
        elif 8 * k == 3 * n:
            c = math.sqrt(0.5)
            tr, ti = (xi - xr) * c, -(xr + xi) * c
        else:
            c, s = math.cos(2 * math.pi * k / n), math.sin(2 * math.pi * k / n)
            tr, ti = xr * c + xi * s, xi * c - xr * s
        out_r[k], out_i[k] = er[k] + tr, ei[k] + ti
        out_r[k + half], out_i[k + half] = er[k] - tr, ei[k] - ti
    return out_r, out_i


def transform_kernel(blocks, radix, rows, *refs):
    hints = refs[:blocks]
    first_ref, twist_ref, table_hi, table_lo, cipher_any, total_ref, out_ref, stage, cipher_ref, sem = refs[blocks:]
    copy = pltpu.make_async_copy(cipher_any, cipher_ref, sem)
    copy.start()
    for top in range(0, rows, 8):
        re, im = [], []
        for u in range(radix):
            lanes = slice(u * LANES, (u + 1) * LANES)
            real = imag = None
            for b in range(blocks):
                h = hints[b][top : top + 8, lanes]
                x, y = h * first_ref[2 * b : 2 * b + 1, lanes], h * first_ref[2 * b + 1 : 2 * b + 2, lanes]
                real = x if real is None else real + x
                imag = y if imag is None else imag + y
            re.append(real)
            im.append(imag)
        re, im = fft_list(re, im)
        for r in range(radix):
            c = twist_ref[2 * r : 2 * r + 1, :]
            s = twist_ref[2 * r + 1 : 2 * r + 2, :]
            at = slice(r * rows + top, r * rows + top + 8)
            stage[at, :LANES] = re[r] * c + im[r] * s
            stage[at, LANES:] = im[r] * c - re[r] * s
    copy.wait()
    for r in range(radix):
        high, low = split_bf16(stage[r * rows : (r + 1) * rows, :])
        dot = functools.partial(jnp.dot, preferred_element_type=jnp.float32)
        spec = dot(high, table_hi[...]) + (dot(low, table_hi[...]) + dot(high, table_lo[...]))
        sr, si = spec[:, :LANES], spec[:, LANES:]
        lanes = slice(r * LANES, (r + 1) * LANES)
        for c in range(2):
            a, b = cipher_ref[2 * c, :, lanes], cipher_ref[2 * c + 1, :, lanes]
            real = jnp.sum(sr * a - si * b, axis=0, keepdims=True)
            imag = jnp.sum(sr * b + si * a, axis=0, keepdims=True)
            out_ref[2 * c : 2 * c + 1, lanes] = total_ref[2 * c : 2 * c + 1, lanes] + real
            out_ref[2 * c + 1 : 2 * c + 2, lanes] = total_ref[2 * c + 1 : 2 * c + 2, lanes] + imag


def transform_products(hints, tables, cipher, total):
    rows, points = hints[0].shape
    radix = points // LANES
    return pl.pallas_call(
        functools.partial(transform_kernel, len(hints), radix, rows),
        out_shape=jax.ShapeDtypeStruct((4, points), jnp.float32),
        in_specs=[pl.BlockSpec(memory_space=pltpu.VMEM)] * (len(hints) + 4)
        + [pl.BlockSpec(memory_space=pl.ANY), pl.BlockSpec(memory_space=pltpu.VMEM)],
        scratch_shapes=[
            pltpu.VMEM((radix * rows, 2 * LANES), jnp.float32),
            pltpu.VMEM((4, rows, points), jnp.float32),
            pltpu.SemaphoreType.DMA,
        ],
        compiler_params=pltpu.CompilerParams(vmem_limit_bytes=16 * MIB),
        cost_estimate=pl.CostEstimate(
            flops=6 * radix * rows * 256 * 256, bytes_accessed=0, transcendentals=0
        ),
    )(*hints, *tables, cipher, total)


def xor_pairs(size, step):
    return [(i, i ^ step) for i in range(size)]


def sum_over(x, axis):
    size = lax.axis_size(axis)
    if size == 4:
        near, far, across = [lax.ppermute(x, axis, xor_pairs(size, step)) for step in (1, 2, 3)]
        return (x + near) + (far + across)
    if size & (size - 1):
        return lax.psum(x, axis)
    step = 1
    while step < size:
        x = x + lax.ppermute(x, axis, xor_pairs(size, step))
        step *= 2
    return x


def line_total(lwe, database, cipher, tables, total):
    own = cipher.shape[1]
    q = own // 4
    h = own - q
    (first,), (far_mid, far_tail) = line_hint(lwe, database, [(0, 3), (1, 1)], [[(0, own)], [(0, h), (h, q)]], 56)
    near = lax.ppermute(first, "col", NEIGHBOURS)
    cross = lax.ppermute(far_mid, "col", CROSS)
    direct = lax.ppermute(far_mid, "col", END_TO_FAR_MIDDLE)
    lwe, database, cipher = lax.optimization_barrier((lwe, database, cipher, first))[:3]
    (kept,), (later,) = line_hint(lwe, database, [(3, 2), (2, 0)], [[(0, own)]] * 2, 32)
    cuts = [(0, 2 * q), (2 * q, q), (h, q)]
    swapped = [swap_digits(cipher, top, rows) for top, rows in cuts]
    near, kept, swapped = lax.optimization_barrier((near, kept, swapped))
    end = at_end()
    round_a = lax.ppermute(later[: 2 * q] + jnp.where(end, 0.0, near[: 2 * q]), "col", ROUND)
    spare = jnp.where(end, far_tail, later[h:] + near[h:])
    piece = later[2 * q : h] + jnp.where(end, 0.0, near[2 * q : h])
    round_b = lax.ppermute(jnp.concatenate([piece, spare], axis=0), "col", ROUND)
    near_tail = lax.ppermute(later[h:], "col", INWARD)
    far_sum = lax.ppermute(far_tail + round_b[q:], "col", CROSS)
    base = kept + jnp.where(end, near, 0.0)
    hint_a = base[: 2 * q] + (cross[: 2 * q] + direct[: 2 * q]) + round_a
    waited, _ = lax.optimization_barrier((round_b, hint_a))
    hint_b = base[2 * q : h] + (cross[2 * q :] + direct[2 * q :]) + waited[:q]
    far_sum, _ = lax.optimization_barrier((far_sum, hint_b))
    with_a = lambda t: transform_products([hint_a, lax.ppermute(hint_a, "row", SWAP)], tables, swapped[0], t)
    hint_c = base[h:] + jnp.where(end, round_b[q:], 0.0) + (near_tail + far_sum)
    total = with_a(total)
    for hint, part in ((hint_b, swapped[1]), (hint_c, swapped[2])):
        total = transform_products([hint, lax.ppermute(hint, "row", SWAP)], tables, part, total)
    return total


def body(parts, database, lwe_matrix, secret_ct):
    row_count, row_rank = lax.axis_size("row"), lax.axis_index("row")
    col_count = lax.axis_size("col")
    points = database.shape[0]
    degree = points * row_count
    radix = points // LANES
    own = secret_ct.shape[3]

    source = (row_rank + jnp.arange(row_count, dtype=jnp.int32)) % row_count if row_count == 2 else jnp.arange(row_count, dtype=jnp.int32)
    index = (source[:, None] * points + jnp.arange(points, dtype=jnp.int32)[None, :]) * (2 * row_rank + 1) % (2 * degree)
    angle = index.astype(jnp.float32) * (np.pi / degree)
    first = jnp.stack([jnp.cos(angle), -jnp.sin(angle)], axis=1).reshape(2 * row_count, points)
    lane = np.arange(LANES)
    turn = 2 * np.pi * (np.arange(radix)[:, None] * lane[None, :] % points) / points
    twist = jnp.asarray(np.stack([np.cos(turn), np.sin(turn)], axis=1).reshape(2 * radix, LANES), jnp.float32)
    small = 2 * np.pi * (lane[:, None] * lane[None, :] % LANES) / LANES
    table = np.block([[np.cos(small), -np.sin(small)], [np.sin(small), np.cos(small)]]).astype(np.float32)
    high = table.astype(jnp.bfloat16)
    low = (table - high.astype(np.float32)).astype(jnp.bfloat16)
    tables = (first, twist, jnp.asarray(high), jnp.asarray(low))

    lwe = lwe_matrix[:, 0, :]
    cipher = secret_ct.reshape(4, own, points)
    total = jnp.zeros((4, points), jnp.float32)
    if col_count == 4 and row_count == 2 and own == LANES and points % 512 == 0:
        total = line_total(lwe, database, cipher, tables, total)
    else:
        swapped = cipher.reshape(4, own, LANES, radix).swapaxes(2, 3).reshape(4, own, points)
        partial = partial_hint(lwe, database, col_count, parts)
        block = own // parts
        for k in range(parts):
            mine = lax.psum_scatter(partial[k], "col", scatter_dimension=0, tiled=True)
            if row_count == 2:
                hints = [mine, lax.ppermute(mine, "row", SWAP)]
            else:
                gathered = lax.all_gather(mine, "row")
                hints = [gathered[b] for b in range(row_count)]
            total = transform_products(hints, tables, swapped[:, k * block : (k + 1) * block], total)
    total = sum_over(sum_over(total, "limb"), "col")
    scale = 1.0 / (math.sqrt(degree) * math.sqrt(2 * lwe_matrix.shape[2]))
    total = total.reshape(4, radix, LANES).swapaxes(1, 2).reshape(2, 2, points)
    return total * scale


def solution(mesh):
    placed = (P(("grp", "row"), "col"), P("col", "limb", None), P(None, None, "limb", "col", "row"))

    def whole(database, lwe_matrix, secret_ct):
        own = lwe_matrix.shape[2] // mesh.shape["col"]
        parts = 2 if own % 16 == 0 else 1
        return jax.shard_map(
            functools.partial(body, parts), mesh=mesh, in_specs=placed, out_specs=P("grp", None, "row"), check_vma=False
        )(database, lwe_matrix, secret_ct)

    return whole
```

```python
import functools
import math

import jax
import jax.numpy as jnp
import numpy as np
from jax import lax
from jax.experimental import pallas as pl
from jax.experimental.pallas import tpu as pltpu
from jax.sharding import PartitionSpec as P

LANES = 128
MIB = 1 << 20
SWAP = [(0, 1), (1, 0)]
INWARD = [(0, 1), (3, 2)]
NEIGHBOURS = [(0, 1), (1, 0), (2, 3), (3, 2)]
END_TO_FAR_MIDDLE = [(0, 2), (3, 1)]
CROSS = [(1, 2), (2, 1)]
ROUND = [(0, 1), (1, 3), (3, 2), (2, 0)]


def split_bf16(x):
    high = x.astype(jnp.bfloat16)
    low = (x - high.astype(jnp.float32)).astype(jnp.bfloat16)
    return high, low


def hint_kernel(groups, parts, block, lwe_ref, data_ref, *rest):
    outs, turned = rest[:-1], rest[-1]

    @pl.when(pl.program_id(0) == 0)
    def _():
        turned[...] = lwe_ref[...].T

    for g in range(groups):
        rows = slice(g * parts * block, (g + 1) * parts * block)
        res = lax.dot_general(
            turned[rows, :], data_ref[...], (((1,), (1,)), ((), ())), preferred_element_type=jnp.float32
        )
        for k in range(parts):
            outs[k][g * block : (g + 1) * block, :] = res[k * block : (k + 1) * block, :]


def partial_hint(lwe, database, groups, parts):
    depth, columns = lwe.shape
    rows = database.shape[0]
    block = columns // (groups * parts)
    tile = min(256, rows)
    return pl.pallas_call(
        functools.partial(hint_kernel, groups, parts, block),
        grid=(rows // tile,),
        in_specs=[
            pl.BlockSpec((depth, columns), lambda i: (0, 0)),
            pl.BlockSpec((tile, depth), lambda i: (i, 0)),
        ],
        out_specs=[pl.BlockSpec((groups * block, tile), lambda i: (0, i))] * parts,
        out_shape=[jax.ShapeDtypeStruct((groups * block, rows), jnp.float32)] * parts,
        scratch_shapes=[pltpu.VMEM((columns, depth), jnp.bfloat16)],
        compiler_params=pltpu.CompilerParams(vmem_limit_bytes=48 * MIB),
        cost_estimate=pl.CostEstimate(
            flops=2 * rows * depth * columns, bytes_accessed=2 * rows * depth, transcendentals=0
        ),
    )(lwe, database)


def at_end():
    z = lax.axis_index("col")
    return jnp.logical_or(z == 0, z == 3)


def role_block(role):
    place = jnp.where(at_end(), role[0], role[1])
    return jnp.where(lax.axis_index("col") >= 2, place, 3 - place)


def line_hint_kernel(roles, cuts, tile, lwe_ref, data_ref, *rest):
    pieces = [(b, top, size) for b, c in enumerate(cuts) for top, size in c]
    outs = rest[: len(pieces)]
    lwe_v, data_v, turned, made, lwe_sem, data_sem, out_sem = rest[len(pieces) :]
    rows = data_ref.shape[0]
    own = made.shape[0] // len(roles)
    lwe_copy = pltpu.make_async_copy(lwe_ref, lwe_v, lwe_sem)
    lwe_copy.start()
    tiles = []
    for i in range(rows // tile):
        at = slice(i * tile, (i + 1) * tile)
        tiles.append(pltpu.make_async_copy(data_ref.at[at, :], data_v.at[at, :], data_sem.at[i]))
    for c in tiles[:1]:
        c.start()
    lwe_copy.wait()
    for c in tiles[1:]:
        c.start()
    for b, role in enumerate(roles):
        at = pl.multiple_of(role_block(role) * own, own)
        turned[b * own : (b + 1) * own, :] = lwe_v[:, pl.ds(at, own)].T
    written = []
    for i, c in enumerate(tiles):
        c.wait()
        at = slice(i * tile, (i + 1) * tile)
        made[:, at] = lax.dot_general(
            turned[...], data_v[at, :], (((1,), (1,)), ((), ())), preferred_element_type=jnp.float32
        )
        for n, (b, top, size) in enumerate(pieces):
            source = made.at[b * own + top : b * own + top + size, at]
            written.append(pltpu.make_async_copy(source, outs[n].at[:, at], out_sem.at[i * len(pieces) + n]))
            written[-1].start()
    for c in written:
        c.wait()


def line_hint(lwe, database, roles, cuts, limit):
    depth, columns = lwe.shape
    rows = database.shape[0]
    own = columns // 4
    tile = min(512, rows)
    flat = pl.pallas_call(
        functools.partial(line_hint_kernel, roles, cuts, tile),
        in_specs=[pl.BlockSpec(memory_space=pl.ANY)] * 2,
        out_shape=[jax.ShapeDtypeStruct((k, rows), jnp.float32) for c in cuts for _, k in c],
        out_specs=[pl.BlockSpec(memory_space=pl.ANY)] * sum(len(c) for c in cuts),
        scratch_shapes=[
            pltpu.VMEM((depth, columns), jnp.bfloat16),
            pltpu.VMEM((rows, depth), jnp.bfloat16),
            pltpu.VMEM((len(roles) * own, depth), jnp.bfloat16),
            pltpu.VMEM((len(roles) * own, rows), jnp.float32),
            pltpu.SemaphoreType.DMA,
            pltpu.SemaphoreType.DMA((rows // tile,)),
            pltpu.SemaphoreType.DMA((rows // tile * sum(len(c) for c in cuts),)),
        ],
        compiler_params=pltpu.CompilerParams(vmem_limit_bytes=limit * MIB),
        cost_estimate=pl.CostEstimate(
            flops=2 * rows * depth * own * len(roles), bytes_accessed=2 * rows * depth, transcendentals=0
        ),
    )(lwe, database)
    out, n = [], 0
    for c in cuts:
        out.append(list(flat[n : n + len(c)]))
        n += len(c)
    return out


def swap_kernel(radix, in_ref, out_ref, stage):
    groups, rows = in_ref.shape[:2]
    some = stage.shape[2] // groups
    for n in range(rows // some):
        at = slice(n * some, (n + 1) * some)
        for k in range(radix):
            lanes = slice(k * LANES, (k + 1) * LANES)
            stage[n, lanes, :] = in_ref[:, at, lanes].reshape(groups * some, LANES).T
        for r in range(radix):
            picked = stage[n, pl.ds(r, LANES, stride=radix), :].T
            out_ref[:, at, r * LANES : (r + 1) * LANES] = picked.reshape(groups, some, LANES)


def swap_digits(cipher, offset, rows):
    points = cipher.shape[2]
    radix = points // LANES
    return pl.pallas_call(
        functools.partial(swap_kernel, radix),
        grid=(1,),
        in_specs=[pl.BlockSpec((4, rows, points), lambda i: (0, offset // rows, 0))],
        out_specs=pl.BlockSpec((4, rows, points), lambda i: (0, 0, 0)),
        out_shape=jax.ShapeDtypeStruct((4, rows, points), jnp.float32),
        scratch_shapes=[pltpu.VMEM((max(1, rows // 32), points, min(4 * rows, LANES)), jnp.float32)],
        compiler_params=pltpu.CompilerParams(vmem_limit_bytes=16 * MIB),
        cost_estimate=pl.CostEstimate(flops=0, bytes_accessed=32 * rows * points, transcendentals=0),
    )(cipher)


def fft_list(re, im):
    n = len(re)
    if n == 1:
        return re, im
    er, ei = fft_list(re[0::2], im[0::2])
    odd_r, odd_i = fft_list(re[1::2], im[1::2])
    half = n // 2
    out_r, out_i = [None] * n, [None] * n
    for k in range(half):
        xr, xi = odd_r[k], odd_i[k]
        if k == 0:
            tr, ti = xr, xi
        elif 4 * k == n:
            tr, ti = xi, -xr
        elif 8 * k == n:
            c = math.sqrt(0.5)
            tr, ti = (xr + xi) * c, (xi - xr) * c
        elif 8 * k == 3 * n:
            c = math.sqrt(0.5)
            tr, ti = (xi - xr) * c, -(xr + xi) * c
        else:
            c, s = math.cos(2 * math.pi * k / n), math.sin(2 * math.pi * k / n)
            tr, ti = xr * c + xi * s, xi * c - xr * s
        out_r[k], out_i[k] = er[k] + tr, ei[k] + ti
        out_r[k + half], out_i[k + half] = er[k] - tr, ei[k] - ti
    return out_r, out_i


def transform_kernel(blocks, radix, rows, *refs):
    hints = refs[:blocks]
    first_ref, twist_ref, table_hi, table_lo, cipher_ref, total_ref, out_ref, stage = refs[blocks:]
    for top in range(0, rows, 8):
        re, im = [], []
        for u in range(radix):
            lanes = slice(u * LANES, (u + 1) * LANES)
            real = imag = None
            for b in range(blocks):
                h = hints[b][top : top + 8, lanes]
                x, y = h * first_ref[2 * b : 2 * b + 1, lanes], h * first_ref[2 * b + 1 : 2 * b + 2, lanes]
                real = x if real is None else real + x
                imag = y if imag is None else imag + y
            re.append(real)
            im.append(imag)
        re, im = fft_list(re, im)
        for r in range(radix):
            c = twist_ref[2 * r : 2 * r + 1, :]
            s = twist_ref[2 * r + 1 : 2 * r + 2, :]
            at = slice(r * rows + top, r * rows + top + 8)
            stage[at, :LANES] = re[r] * c + im[r] * s
            stage[at, LANES:] = im[r] * c - re[r] * s
    for r in range(radix):
        high, low = split_bf16(stage[r * rows : (r + 1) * rows, :])
        dot = functools.partial(jnp.dot, preferred_element_type=jnp.float32)
        spec = dot(high, table_hi[...]) + (dot(low, table_hi[...]) + dot(high, table_lo[...]))
        sr, si = spec[:, :LANES], spec[:, LANES:]
        lanes = slice(r * LANES, (r + 1) * LANES)
        for c in range(2):
            a, b = cipher_ref[2 * c, :, lanes], cipher_ref[2 * c + 1, :, lanes]
            real = jnp.sum(sr * a - si * b, axis=0, keepdims=True)
            imag = jnp.sum(sr * b + si * a, axis=0, keepdims=True)
            out_ref[2 * c : 2 * c + 1, lanes] = total_ref[2 * c : 2 * c + 1, lanes] + real
            out_ref[2 * c + 1 : 2 * c + 2, lanes] = total_ref[2 * c + 1 : 2 * c + 2, lanes] + imag


def transform_products(hints, tables, cipher, total):
    rows, points = hints[0].shape
    radix = points // LANES
    return pl.pallas_call(
        functools.partial(transform_kernel, len(hints), radix, rows),
        out_shape=jax.ShapeDtypeStruct((4, points), jnp.float32),
        in_specs=[pl.BlockSpec(memory_space=pltpu.VMEM)] * (len(hints) + 6),
        out_specs=pl.BlockSpec(memory_space=pltpu.VMEM),
        scratch_shapes=[
            pltpu.VMEM((radix * rows, 2 * LANES), jnp.float32),
        ],
        compiler_params=pltpu.CompilerParams(vmem_limit_bytes=16 * MIB),
        cost_estimate=pl.CostEstimate(
            flops=6 * radix * rows * 256 * 256, bytes_accessed=24 * rows * points, transcendentals=0
        ),
    )(*hints, *tables, cipher, total)


def xor_pairs(size, step):
    return [(i, i ^ step) for i in range(size)]


def sum_over(x, axis):
    size = lax.axis_size(axis)
    if size == 4:
        near, far, across = [lax.ppermute(x, axis, xor_pairs(size, step)) for step in (1, 2, 3)]
        return (x + near) + (far + across)
    if size & (size - 1):
        return lax.psum(x, axis)
    step = 1
    while step < size:
        x = x + lax.ppermute(x, axis, xor_pairs(size, step))
        step *= 2
    return x


def line_total(lwe, database, cipher, tables, total):
    own = cipher.shape[1]
    q = own // 4
    h = own - q
    (first,), (far_mid, far_tail) = line_hint(lwe, database, [(0, 3), (1, 1)], [[(0, own)], [(0, h), (h, q)]], 56)
    near = lax.ppermute(first, "col", NEIGHBOURS)
    cross = lax.ppermute(far_mid, "col", CROSS)
    direct = lax.ppermute(far_mid, "col", END_TO_FAR_MIDDLE)
    lwe, database, cipher = lax.optimization_barrier((lwe, database, cipher, first))[:3]
    (kept,), (later,) = line_hint(lwe, database, [(3, 2), (2, 0)], [[(0, own)]] * 2, 32)
    cuts = [(0, 2 * q), (2 * q, q), (h, q)]
    swapped = [swap_digits(cipher, top, rows) for top, rows in cuts]
    near, kept, swapped = lax.optimization_barrier((near, kept, swapped))
    end = at_end()
    round_a = lax.ppermute(later[: 2 * q] + jnp.where(end, 0.0, near[: 2 * q]), "col", ROUND)
    spare = jnp.where(end, far_tail, later[h:] + near[h:])
    piece = later[2 * q : h] + jnp.where(end, 0.0, near[2 * q : h])
    round_b = lax.ppermute(jnp.concatenate([piece, spare], axis=0), "col", ROUND)
    near_tail = lax.ppermute(later[h:], "col", INWARD)
    far_sum = lax.ppermute(far_tail + round_b[q:], "col", CROSS)
    base = kept + jnp.where(end, near, 0.0)
    hint_a = base[: 2 * q] + (cross[: 2 * q] + direct[: 2 * q]) + round_a
    waited, _ = lax.optimization_barrier((round_b, hint_a))
    hint_b = base[2 * q : h] + (cross[2 * q :] + direct[2 * q :]) + waited[:q]
    far_sum, _ = lax.optimization_barrier((far_sum, hint_b))
    with_a = lambda t: transform_products([hint_a, lax.ppermute(hint_a, "row", SWAP)], tables, swapped[0], t)
    hint_c = base[h:] + jnp.where(end, round_b[q:], 0.0) + (near_tail + far_sum)
    total = with_a(total)
    for hint, part in ((hint_b, swapped[1]), (hint_c, swapped[2])):
        total = transform_products([hint, lax.ppermute(hint, "row", SWAP)], tables, part, total)
    return total


def body(parts, database, lwe_matrix, secret_ct):
    row_count, row_rank = lax.axis_size("row"), lax.axis_index("row")
    col_count = lax.axis_size("col")
    points = database.shape[0]
    degree = points * row_count
    radix = points // LANES
    own = secret_ct.shape[3]

    source = (row_rank + jnp.arange(row_count, dtype=jnp.int32)) % row_count if row_count == 2 else jnp.arange(row_count, dtype=jnp.int32)
    index = (source[:, None] * points + jnp.arange(points, dtype=jnp.int32)[None, :]) * (2 * row_rank + 1) % (2 * degree)
    angle = index.astype(jnp.float32) * (np.pi / degree)
    first = jnp.stack([jnp.cos(angle), -jnp.sin(angle)], axis=1).reshape(2 * row_count, points)
    lane = np.arange(LANES)
    turn = 2 * np.pi * (np.arange(radix)[:, None] * lane[None, :] % points) / points
    twist = jnp.asarray(np.stack([np.cos(turn), np.sin(turn)], axis=1).reshape(2 * radix, LANES), jnp.float32)
    small = 2 * np.pi * (lane[:, None] * lane[None, :] % LANES) / LANES
    table = np.block([[np.cos(small), -np.sin(small)], [np.sin(small), np.cos(small)]]).astype(np.float32)
    high = table.astype(jnp.bfloat16)
    low = (table - high.astype(np.float32)).astype(jnp.bfloat16)
    tables = (first, twist, jnp.asarray(high), jnp.asarray(low))

    lwe = lwe_matrix[:, 0, :]
    cipher = secret_ct.reshape(4, own, points)
    total = jnp.zeros((4, points), jnp.float32)
    if col_count == 4 and row_count == 2 and own == LANES and points % 512 == 0:
        total = line_total(lwe, database, cipher, tables, total)
    else:
        swapped = cipher.reshape(4, own, LANES, radix).swapaxes(2, 3).reshape(4, own, points)
        partial = partial_hint(lwe, database, col_count, parts)
        block = own // parts
        for k in range(parts):
            mine = lax.psum_scatter(partial[k], "col", scatter_dimension=0, tiled=True)
            if row_count == 2:
                hints = [mine, lax.ppermute(mine, "row", SWAP)]
            else:
                gathered = lax.all_gather(mine, "row")
                hints = [gathered[b] for b in range(row_count)]
            total = transform_products(hints, tables, swapped[:, k * block : (k + 1) * block], total)
    total = sum_over(sum_over(total, "limb"), "col")
    scale = 1.0 / (math.sqrt(degree) * math.sqrt(2 * lwe_matrix.shape[2]))
    total = total.reshape(4, radix, LANES).swapaxes(1, 2).reshape(2, 2, points)
    return total * scale


def solution(mesh):
    placed = (P(("grp", "row"), "col"), P("col", "limb", None), P(None, None, "limb", "col", "row"))

    def whole(database, lwe_matrix, secret_ct):
        own = lwe_matrix.shape[2] // mesh.shape["col"]
        parts = 2 if own % 16 == 0 else 1
        return jax.shard_map(
            functools.partial(body, parts), mesh=mesh, in_specs=placed, out_specs=P("grp", None, "row"), check_vma=False
        )(database, lwe_matrix, secret_ct)

    return whole
```

```python
import functools
import math

import jax
import jax.numpy as jnp
import numpy as np
from jax import lax
from jax.experimental import pallas as pl
from jax.experimental.pallas import tpu as pltpu
from jax.sharding import PartitionSpec as P

LANES = 128
MIB = 1 << 20
SWAP = [(0, 1), (1, 0)]
INWARD = [(0, 1), (3, 2)]
NEIGHBOURS = [(0, 1), (1, 0), (2, 3), (3, 2)]
END_TO_FAR_MIDDLE = [(0, 2), (3, 1)]
CROSS = [(1, 2), (2, 1)]
ROUND = [(0, 1), (1, 3), (3, 2), (2, 0)]


def split_bf16(x):
    high = x.astype(jnp.bfloat16)
    low = (x - high.astype(jnp.float32)).astype(jnp.bfloat16)
    return high, low


def hint_kernel(groups, parts, block, lwe_ref, data_ref, *rest):
    outs, turned = rest[:-1], rest[-1]

    @pl.when(pl.program_id(0) == 0)
    def _():
        turned[...] = lwe_ref[...].T

    for g in range(groups):
        rows = slice(g * parts * block, (g + 1) * parts * block)
        res = lax.dot_general(
            turned[rows, :], data_ref[...], (((1,), (1,)), ((), ())), preferred_element_type=jnp.float32
        )
        for k in range(parts):
            outs[k][g * block : (g + 1) * block, :] = res[k * block : (k + 1) * block, :]


def partial_hint(lwe, database, groups, parts):
    depth, columns = lwe.shape
    rows = database.shape[0]
    block = columns // (groups * parts)
    tile = min(256, rows)
    return pl.pallas_call(
        functools.partial(hint_kernel, groups, parts, block),
        grid=(rows // tile,),
        in_specs=[
            pl.BlockSpec((depth, columns), lambda i: (0, 0)),
            pl.BlockSpec((tile, depth), lambda i: (i, 0)),
        ],
        out_specs=[pl.BlockSpec((groups * block, tile), lambda i: (0, i))] * parts,
        out_shape=[jax.ShapeDtypeStruct((groups * block, rows), jnp.float32)] * parts,
        scratch_shapes=[pltpu.VMEM((columns, depth), jnp.bfloat16)],
        compiler_params=pltpu.CompilerParams(vmem_limit_bytes=48 * MIB),
        cost_estimate=pl.CostEstimate(
            flops=2 * rows * depth * columns, bytes_accessed=2 * rows * depth, transcendentals=0
        ),
    )(lwe, database)


def at_end():
    z = lax.axis_index("col")
    return jnp.logical_or(z == 0, z == 3)


def role_block(role):
    place = jnp.where(at_end(), role[0], role[1])
    return jnp.where(lax.axis_index("col") >= 2, place, 3 - place)


def line_hint_kernel(roles, cuts, tile, lwe_ref, data_ref, *rest):
    pieces = [(b, top, size) for b, c in enumerate(cuts) for top, size in c]
    outs = rest[: len(pieces)]
    lwe_v, data_v, turned, made, lwe_sem, data_sem, out_sem = rest[len(pieces) :]
    rows = data_ref.shape[0]
    own = made.shape[0] // len(roles)
    lwe_copy = pltpu.make_async_copy(lwe_ref, lwe_v, lwe_sem)
    lwe_copy.start()
    tiles = []
    for i in range(rows // tile):
        at = slice(i * tile, (i + 1) * tile)
        tiles.append(pltpu.make_async_copy(data_ref.at[at, :], data_v.at[at, :], data_sem.at[i]))
    for c in tiles[:1]:
        c.start()
    lwe_copy.wait()
    for c in tiles[1:]:
        c.start()
    for b, role in enumerate(roles):
        at = pl.multiple_of(role_block(role) * own, own)
        turned[b * own : (b + 1) * own, :] = lwe_v[:, pl.ds(at, own)].T
    written = []
    for i, c in enumerate(tiles):
        c.wait()
        at = slice(i * tile, (i + 1) * tile)
        made[:, at] = lax.dot_general(
            turned[...], data_v[at, :], (((1,), (1,)), ((), ())), preferred_element_type=jnp.float32
        )
        for n, (b, top, size) in enumerate(pieces):
            source = made.at[b * own + top : b * own + top + size, at]
            written.append(pltpu.make_async_copy(source, outs[n].at[:, at], out_sem.at[i * len(pieces) + n]))
            written[-1].start()
    for c in written:
        c.wait()


def line_hint(lwe, database, roles, cuts, limit):
    depth, columns = lwe.shape
    rows = database.shape[0]
    own = columns // 4
    tile = min(512, rows)
    flat = pl.pallas_call(
        functools.partial(line_hint_kernel, roles, cuts, tile),
        in_specs=[pl.BlockSpec(memory_space=pl.ANY)] * 2,
        out_shape=[jax.ShapeDtypeStruct((k, rows), jnp.float32) for c in cuts for _, k in c],
        out_specs=[pl.BlockSpec(memory_space=pl.ANY)] * sum(len(c) for c in cuts),
        scratch_shapes=[
            pltpu.VMEM((depth, columns), jnp.bfloat16),
            pltpu.VMEM((rows, depth), jnp.bfloat16),
            pltpu.VMEM((len(roles) * own, depth), jnp.bfloat16),
            pltpu.VMEM((len(roles) * own, rows), jnp.float32),
            pltpu.SemaphoreType.DMA,
            pltpu.SemaphoreType.DMA((rows // tile,)),
            pltpu.SemaphoreType.DMA((rows // tile * sum(len(c) for c in cuts),)),
        ],
        compiler_params=pltpu.CompilerParams(vmem_limit_bytes=limit * MIB),
        cost_estimate=pl.CostEstimate(
            flops=2 * rows * depth * own * len(roles), bytes_accessed=2 * rows * depth, transcendentals=0
        ),
    )(lwe, database)
    out, n = [], 0
    for c in cuts:
        out.append(list(flat[n : n + len(c)]))
        n += len(c)
    return out


def swap_kernel(radix, in_ref, out_ref, stage):
    groups, rows = in_ref.shape[:2]
    some = stage.shape[2] // groups
    for n in range(rows // some):
        at = slice(n * some, (n + 1) * some)
        for k in range(radix):
            lanes = slice(k * LANES, (k + 1) * LANES)
            stage[n, lanes, :] = in_ref[:, at, lanes].reshape(groups * some, LANES).T
        for r in range(radix):
            picked = stage[n, pl.ds(r, LANES, stride=radix), :].T
            out_ref[:, at, r * LANES : (r + 1) * LANES] = picked.reshape(groups, some, LANES)


def swap_digits(cipher, offset, rows):
    points = cipher.shape[2]
    radix = points // LANES
    return pl.pallas_call(
        functools.partial(swap_kernel, radix),
        grid=(1,),
        in_specs=[pl.BlockSpec((4, rows, points), lambda i: (0, offset // rows, 0))],
        out_specs=pl.BlockSpec((4, rows, points), lambda i: (0, 0, 0)),
        out_shape=jax.ShapeDtypeStruct((4, rows, points), jnp.float32),
        scratch_shapes=[pltpu.VMEM((max(1, rows // 32), points, min(4 * rows, LANES)), jnp.float32)],
        compiler_params=pltpu.CompilerParams(vmem_limit_bytes=16 * MIB),
        cost_estimate=pl.CostEstimate(flops=0, bytes_accessed=32 * rows * points, transcendentals=0),
    )(cipher)


def fft_list(re, im):
    n = len(re)
    if n == 1:
        return re, im
    er, ei = fft_list(re[0::2], im[0::2])
    odd_r, odd_i = fft_list(re[1::2], im[1::2])
    half = n // 2
    out_r, out_i = [None] * n, [None] * n
    for k in range(half):
        xr, xi = odd_r[k], odd_i[k]
        if k == 0:
            tr, ti = xr, xi
        elif 4 * k == n:
            tr, ti = xi, -xr
        elif 8 * k == n:
            c = math.sqrt(0.5)
            tr, ti = (xr + xi) * c, (xi - xr) * c
        elif 8 * k == 3 * n:
            c = math.sqrt(0.5)
            tr, ti = (xi - xr) * c, -(xr + xi) * c
        else:
            c, s = math.cos(2 * math.pi * k / n), math.sin(2 * math.pi * k / n)
            tr, ti = xr * c + xi * s, xi * c - xr * s
        out_r[k], out_i[k] = er[k] + tr, ei[k] + ti
        out_r[k + half], out_i[k + half] = er[k] - tr, ei[k] - ti
    return out_r, out_i


def transform_kernel(blocks, radix, rows, *refs):
    hints = refs[:blocks]
    first_ref, twist_ref, table_hi, table_lo, cipher_ref, total_ref, out_ref, stage = refs[blocks:]
    for top in range(0, rows, 8):
        re, im = [], []
        for u in range(radix):
            lanes = slice(u * LANES, (u + 1) * LANES)
            real = imag = None
            for b in range(blocks):
                h = hints[b][top : top + 8, lanes]
                x, y = h * first_ref[2 * b : 2 * b + 1, lanes], h * first_ref[2 * b + 1 : 2 * b + 2, lanes]
                real = x if real is None else real + x
                imag = y if imag is None else imag + y
            re.append(real)
            im.append(imag)
        re, im = fft_list(re, im)
        for r in range(radix):
            c = twist_ref[2 * r : 2 * r + 1, :]
            s = twist_ref[2 * r + 1 : 2 * r + 2, :]
            at = slice(r * rows + top, r * rows + top + 8)
            stage[at, :LANES] = re[r] * c + im[r] * s
            stage[at, LANES:] = im[r] * c - re[r] * s
    for r in range(radix):
        high, low = split_bf16(stage[r * rows : (r + 1) * rows, :])
        dot = functools.partial(jnp.dot, preferred_element_type=jnp.float32)
        spec = dot(high, table_hi[...]) + (dot(low, table_hi[...]) + dot(high, table_lo[...]))
        sr, si = spec[:, :LANES], spec[:, LANES:]
        lanes = slice(r * LANES, (r + 1) * LANES)
        for c in range(2):
            a, b = cipher_ref[2 * c, :, lanes], cipher_ref[2 * c + 1, :, lanes]
            real = jnp.sum(sr * a - si * b, axis=0, keepdims=True)
            imag = jnp.sum(sr * b + si * a, axis=0, keepdims=True)
            out_ref[2 * c : 2 * c + 1, lanes] = total_ref[2 * c : 2 * c + 1, lanes] + real
            out_ref[2 * c + 1 : 2 * c + 2, lanes] = total_ref[2 * c + 1 : 2 * c + 2, lanes] + imag


def transform_products(hints, tables, cipher, total):
    rows, points = hints[0].shape
    radix = points // LANES
    return pl.pallas_call(
        functools.partial(transform_kernel, len(hints), radix, rows),
        out_shape=jax.ShapeDtypeStruct((4, points), jnp.float32),
        in_specs=[pl.BlockSpec(memory_space=pltpu.VMEM)] * (len(hints) + 6),
        out_specs=pl.BlockSpec(memory_space=pltpu.VMEM),
        scratch_shapes=[
            pltpu.VMEM((radix * rows, 2 * LANES), jnp.float32),
        ],
        compiler_params=pltpu.CompilerParams(vmem_limit_bytes=16 * MIB),
        cost_estimate=pl.CostEstimate(
            flops=6 * radix * rows * 256 * 256, bytes_accessed=24 * rows * points, transcendentals=0
        ),
    )(*hints, *tables, cipher, total)


def xor_pairs(size, step):
    return [(i, i ^ step) for i in range(size)]


def sum_over(x, axis):
    size = lax.axis_size(axis)
    if size == 4:
        near, far, across = [lax.ppermute(x, axis, xor_pairs(size, step)) for step in (1, 2, 3)]
        return (x + near) + (far + across)
    if size & (size - 1):
        return lax.psum(x, axis)
    step = 1
    while step < size:
        x = x + lax.ppermute(x, axis, xor_pairs(size, step))
        step *= 2
    return x


def line_total(lwe, database, cipher, tables, total):
    own = cipher.shape[1]
    q = own // 4
    h = own - q
    (first,), (far_mid, far_tail) = line_hint(lwe, database, [(0, 3), (1, 1)], [[(0, own)], [(0, h), (h, q)]], 56)
    near = lax.ppermute(first, "col", NEIGHBOURS)
    cross = lax.ppermute(far_mid, "col", CROSS)
    direct = lax.ppermute(far_mid, "col", END_TO_FAR_MIDDLE)
    lwe, database, cipher = lax.optimization_barrier((lwe, database, cipher, first))[:3]
    (kept,), (later,) = line_hint(lwe, database, [(3, 2), (2, 0)], [[(0, own)]] * 2, 32)
    cuts = [(0, 2 * q), (2 * q, q), (h, q)]
    swapped = [swap_digits(cipher, top, rows) for top, rows in cuts]
    near, kept, swapped = lax.optimization_barrier((near, kept, swapped))
    end = at_end()
    round_a = lax.ppermute(later[: 2 * q] + jnp.where(end, 0.0, near[: 2 * q]), "col", ROUND)
    spare = jnp.where(end, far_tail, later[h:] + near[h:])
    piece = later[2 * q : h] + jnp.where(end, 0.0, near[2 * q : h])
    round_b = lax.ppermute(jnp.concatenate([piece, spare], axis=0), "col", ROUND)
    near_tail = lax.ppermute(later[h:], "col", INWARD)
    far_sum = lax.ppermute(far_tail + round_b[q:], "col", CROSS)
    base = kept + jnp.where(end, near, 0.0)
    hint_a = base[: 2 * q] + (cross[: 2 * q] + direct[: 2 * q]) + round_a
    waited, _ = lax.optimization_barrier((round_b, hint_a))
    hint_b = base[2 * q : h] + (cross[2 * q :] + direct[2 * q :]) + waited[:q]
    far_sum, _ = lax.optimization_barrier((far_sum, hint_b))
    with_a = lambda t: transform_products([hint_a, lax.ppermute(hint_a, "row", SWAP)], tables, swapped[0], t)
    total = with_a(total)
    far_sum, total = lax.optimization_barrier((far_sum, total))
    hint_c = base[h:] + jnp.where(end, round_b[q:], 0.0) + (near_tail + far_sum)
    for hint, part in ((hint_b, swapped[1]), (hint_c, swapped[2])):
        total = transform_products([hint, lax.ppermute(hint, "row", SWAP)], tables, part, total)
    return total


def body(parts, database, lwe_matrix, secret_ct):
    row_count, row_rank = lax.axis_size("row"), lax.axis_index("row")
    col_count = lax.axis_size("col")
    points = database.shape[0]
    degree = points * row_count
    radix = points // LANES
    own = secret_ct.shape[3]

    source = (row_rank + jnp.arange(row_count, dtype=jnp.int32)) % row_count if row_count == 2 else jnp.arange(row_count, dtype=jnp.int32)
    index = (source[:, None] * points + jnp.arange(points, dtype=jnp.int32)[None, :]) * (2 * row_rank + 1) % (2 * degree)
    angle = index.astype(jnp.float32) * (np.pi / degree)
    first = jnp.stack([jnp.cos(angle), -jnp.sin(angle)], axis=1).reshape(2 * row_count, points)
    lane = np.arange(LANES)
    turn = 2 * np.pi * (np.arange(radix)[:, None] * lane[None, :] % points) / points
    twist = jnp.asarray(np.stack([np.cos(turn), np.sin(turn)], axis=1).reshape(2 * radix, LANES), jnp.float32)
    small = 2 * np.pi * (lane[:, None] * lane[None, :] % LANES) / LANES
    table = np.block([[np.cos(small), -np.sin(small)], [np.sin(small), np.cos(small)]]).astype(np.float32)
    high = table.astype(jnp.bfloat16)
    low = (table - high.astype(np.float32)).astype(jnp.bfloat16)
    tables = (first, twist, jnp.asarray(high), jnp.asarray(low))

    lwe = lwe_matrix[:, 0, :]
    cipher = secret_ct.reshape(4, own, points)
    total = jnp.zeros((4, points), jnp.float32)
    if col_count == 4 and row_count == 2 and own == LANES and points % 512 == 0:
        total = line_total(lwe, database, cipher, tables, total)
    else:
        swapped = cipher.reshape(4, own, LANES, radix).swapaxes(2, 3).reshape(4, own, points)
        partial = partial_hint(lwe, database, col_count, parts)
        block = own // parts
        for k in range(parts):
            mine = lax.psum_scatter(partial[k], "col", scatter_dimension=0, tiled=True)
            if row_count == 2:
                hints = [mine, lax.ppermute(mine, "row", SWAP)]
            else:
                gathered = lax.all_gather(mine, "row")
                hints = [gathered[b] for b in range(row_count)]
            total = transform_products(hints, tables, swapped[:, k * block : (k + 1) * block], total)
    total = sum_over(sum_over(total, "limb"), "col")
    scale = 1.0 / (math.sqrt(degree) * math.sqrt(2 * lwe_matrix.shape[2]))
    total = total.reshape(4, radix, LANES).swapaxes(1, 2).reshape(2, 2, points)
    return total * scale


def solution(mesh):
    placed = (P(("grp", "row"), "col"), P("col", "limb", None), P(None, None, "limb", "col", "row"))

    def whole(database, lwe_matrix, secret_ct):
        own = lwe_matrix.shape[2] // mesh.shape["col"]
        parts = 2 if own % 16 == 0 else 1
        return jax.shard_map(
            functools.partial(body, parts), mesh=mesh, in_specs=placed, out_specs=P("grp", None, "row"), check_vma=False
        )(database, lwe_matrix, secret_ct)

    return whole
```

```python
import functools
import math

import jax
import jax.numpy as jnp
import numpy as np
from jax import lax
from jax.experimental import pallas as pl
from jax.experimental.pallas import tpu as pltpu
from jax.sharding import PartitionSpec as P

LANES = 128
MIB = 1 << 20
SWAP = [(0, 1), (1, 0)]
INWARD = [(0, 1), (3, 2)]
NEIGHBOURS = [(0, 1), (1, 0), (2, 3), (3, 2)]
END_TO_FAR_MIDDLE = [(0, 2), (3, 1)]
CROSS = [(1, 2), (2, 1)]
ROUND = [(0, 1), (1, 3), (3, 2), (2, 0)]


def split_bf16(x):
    high = x.astype(jnp.bfloat16)
    low = (x - high.astype(jnp.float32)).astype(jnp.bfloat16)
    return high, low


def hint_kernel(groups, parts, block, lwe_ref, data_ref, *rest):
    outs, turned = rest[:-1], rest[-1]

    @pl.when(pl.program_id(0) == 0)
    def _():
        turned[...] = lwe_ref[...].T

    for g in range(groups):
        rows = slice(g * parts * block, (g + 1) * parts * block)
        res = lax.dot_general(
            turned[rows, :], data_ref[...], (((1,), (1,)), ((), ())), preferred_element_type=jnp.float32
        )
        for k in range(parts):
            outs[k][g * block : (g + 1) * block, :] = res[k * block : (k + 1) * block, :]


def partial_hint(lwe, database, groups, parts):
    depth, columns = lwe.shape
    rows = database.shape[0]
    block = columns // (groups * parts)
    tile = min(256, rows)
    return pl.pallas_call(
        functools.partial(hint_kernel, groups, parts, block),
        grid=(rows // tile,),
        in_specs=[
            pl.BlockSpec((depth, columns), lambda i: (0, 0)),
            pl.BlockSpec((tile, depth), lambda i: (i, 0)),
        ],
        out_specs=[pl.BlockSpec((groups * block, tile), lambda i: (0, i))] * parts,
        out_shape=[jax.ShapeDtypeStruct((groups * block, rows), jnp.float32)] * parts,
        scratch_shapes=[pltpu.VMEM((columns, depth), jnp.bfloat16)],
        compiler_params=pltpu.CompilerParams(vmem_limit_bytes=48 * MIB),
        cost_estimate=pl.CostEstimate(
            flops=2 * rows * depth * columns, bytes_accessed=2 * rows * depth, transcendentals=0
        ),
    )(lwe, database)


def at_end():
    z = lax.axis_index("col")
    return jnp.logical_or(z == 0, z == 3)


def role_block(role):
    place = jnp.where(at_end(), role[0], role[1])
    return jnp.where(lax.axis_index("col") >= 2, place, 3 - place)


def line_hint_kernel(roles, cuts, tile, lwe_ref, data_ref, *rest):
    pieces = [(b, top, size) for b, c in enumerate(cuts) for top, size in c]
    outs = rest[: len(pieces)]
    lwe_v, data_v, turned, made, lwe_sem, data_sem, out_sem = rest[len(pieces) :]
    rows = data_ref.shape[0]
    own = made.shape[0] // len(roles)
    share = lwe_ref.shape[0] // 4
    lwe_copies = []
    for i in range(4):
        at = slice(i * share, (i + 1) * share)
        lwe_copies.append(pltpu.make_async_copy(lwe_ref.at[at, :], lwe_v.at[at, :], lwe_sem.at[i]))
        lwe_copies[-1].start()
    tiles = []
    for i in range(rows // tile):
        at = slice(i * tile, (i + 1) * tile)
        tiles.append(pltpu.make_async_copy(data_ref.at[at, :], data_v.at[at, :], data_sem.at[i]))
    for c in tiles[:1]:
        c.start()
    for c in lwe_copies:
        c.wait()
    for c in tiles[1:]:
        c.start()
    for b, role in enumerate(roles):
        at = pl.multiple_of(role_block(role) * own, own)
        turned[b * own : (b + 1) * own, :] = lwe_v[:, pl.ds(at, own)].T
    written = []
    for i, c in enumerate(tiles):
        c.wait()
        at = slice(i * tile, (i + 1) * tile)
        made[:, at] = lax.dot_general(
            turned[...], data_v[at, :], (((1,), (1,)), ((), ())), preferred_element_type=jnp.float32
        )
        for n, (b, top, size) in enumerate(pieces):
            source = made.at[b * own + top : b * own + top + size, at]
            written.append(pltpu.make_async_copy(source, outs[n].at[:, at], out_sem.at[i * len(pieces) + n]))
            written[-1].start()
    for c in written:
        c.wait()


def line_hint(lwe, database, roles, cuts, limit):
    depth, columns = lwe.shape
    rows = database.shape[0]
    own = columns // 4
    tile = min(512, rows)
    flat = pl.pallas_call(
        functools.partial(line_hint_kernel, roles, cuts, tile),
        in_specs=[pl.BlockSpec(memory_space=pl.ANY)] * 2,
        out_shape=[jax.ShapeDtypeStruct((k, rows), jnp.float32) for c in cuts for _, k in c],
        out_specs=[pl.BlockSpec(memory_space=pl.ANY)] * sum(len(c) for c in cuts),
        scratch_shapes=[
            pltpu.VMEM((depth, columns), jnp.bfloat16),
            pltpu.VMEM((rows, depth), jnp.bfloat16),
            pltpu.VMEM((len(roles) * own, depth), jnp.bfloat16),
            pltpu.VMEM((len(roles) * own, rows), jnp.float32),
            pltpu.SemaphoreType.DMA((4,)),
            pltpu.SemaphoreType.DMA((rows // tile,)),
            pltpu.SemaphoreType.DMA((rows // tile * sum(len(c) for c in cuts),)),
        ],
        compiler_params=pltpu.CompilerParams(vmem_limit_bytes=limit * MIB),
        cost_estimate=pl.CostEstimate(
            flops=2 * rows * depth * own * len(roles), bytes_accessed=2 * rows * depth, transcendentals=0
        ),
    )(lwe, database)
    out, n = [], 0
    for c in cuts:
        out.append(list(flat[n : n + len(c)]))
        n += len(c)
    return out


def swap_kernel(radix, in_ref, out_ref, stage):
    groups, rows = in_ref.shape[:2]
    some = stage.shape[2] // groups
    for n in range(rows // some):
        at = slice(n * some, (n + 1) * some)
        for k in range(radix):
            lanes = slice(k * LANES, (k + 1) * LANES)
            stage[n, lanes, :] = in_ref[:, at, lanes].reshape(groups * some, LANES).T
        for r in range(radix):
            picked = stage[n, pl.ds(r, LANES, stride=radix), :].T
            out_ref[:, at, r * LANES : (r + 1) * LANES] = picked.reshape(groups, some, LANES)


def swap_digits(cipher, offset, rows):
    points = cipher.shape[2]
    radix = points // LANES
    return pl.pallas_call(
        functools.partial(swap_kernel, radix),
        grid=(1,),
        in_specs=[pl.BlockSpec((4, rows, points), lambda i: (0, offset // rows, 0))],
        out_specs=pl.BlockSpec((4, rows, points), lambda i: (0, 0, 0)),
        out_shape=jax.ShapeDtypeStruct((4, rows, points), jnp.float32),
        scratch_shapes=[pltpu.VMEM((max(1, rows // 32), points, min(4 * rows, LANES)), jnp.float32)],
        compiler_params=pltpu.CompilerParams(vmem_limit_bytes=16 * MIB),
        cost_estimate=pl.CostEstimate(flops=0, bytes_accessed=32 * rows * points, transcendentals=0),
    )(cipher)


def fft_list(re, im):
    n = len(re)
    if n == 1:
        return re, im
    er, ei = fft_list(re[0::2], im[0::2])
    odd_r, odd_i = fft_list(re[1::2], im[1::2])
    half = n // 2
    out_r, out_i = [None] * n, [None] * n
    for k in range(half):
        xr, xi = odd_r[k], odd_i[k]
        if k == 0:
            tr, ti = xr, xi
        elif 4 * k == n:
            tr, ti = xi, -xr
        elif 8 * k == n:
            c = math.sqrt(0.5)
            tr, ti = (xr + xi) * c, (xi - xr) * c
        elif 8 * k == 3 * n:
            c = math.sqrt(0.5)
            tr, ti = (xi - xr) * c, -(xr + xi) * c
        else:
            c, s = math.cos(2 * math.pi * k / n), math.sin(2 * math.pi * k / n)
            tr, ti = xr * c + xi * s, xi * c - xr * s
        out_r[k], out_i[k] = er[k] + tr, ei[k] + ti
        out_r[k + half], out_i[k + half] = er[k] - tr, ei[k] - ti
    return out_r, out_i


def transform_kernel(blocks, radix, rows, *refs):
    hints = refs[:blocks]
    first_ref, twist_ref, table_hi, table_lo, cipher_ref, total_ref, out_ref, stage = refs[blocks:]
    for top in range(0, rows, 8):
        re, im = [], []
        for u in range(radix):
            lanes = slice(u * LANES, (u + 1) * LANES)
            real = imag = None
            for b in range(blocks):
                h = hints[b][top : top + 8, lanes]
                x, y = h * first_ref[2 * b : 2 * b + 1, lanes], h * first_ref[2 * b + 1 : 2 * b + 2, lanes]
                real = x if real is None else real + x
                imag = y if imag is None else imag + y
            re.append(real)
            im.append(imag)
        re, im = fft_list(re, im)
        for r in range(radix):
            c = twist_ref[2 * r : 2 * r + 1, :]
            s = twist_ref[2 * r + 1 : 2 * r + 2, :]
            at = slice(r * rows + top, r * rows + top + 8)
            stage[at, :LANES] = re[r] * c + im[r] * s
            stage[at, LANES:] = im[r] * c - re[r] * s
    for r in range(radix):
        high, low = split_bf16(stage[r * rows : (r + 1) * rows, :])
        dot = functools.partial(jnp.dot, preferred_element_type=jnp.float32)
        spec = dot(high, table_hi[...]) + (dot(low, table_hi[...]) + dot(high, table_lo[...]))
        sr, si = spec[:, :LANES], spec[:, LANES:]
        lanes = slice(r * LANES, (r + 1) * LANES)
        for c in range(2):
            a, b = cipher_ref[2 * c, :, lanes], cipher_ref[2 * c + 1, :, lanes]
            real = jnp.sum(sr * a - si * b, axis=0, keepdims=True)
            imag = jnp.sum(sr * b + si * a, axis=0, keepdims=True)
            out_ref[2 * c : 2 * c + 1, lanes] = total_ref[2 * c : 2 * c + 1, lanes] + real
            out_ref[2 * c + 1 : 2 * c + 2, lanes] = total_ref[2 * c + 1 : 2 * c + 2, lanes] + imag


def transform_products(hints, tables, cipher, total):
    rows, points = hints[0].shape
    radix = points // LANES
    return pl.pallas_call(
        functools.partial(transform_kernel, len(hints), radix, rows),
        out_shape=jax.ShapeDtypeStruct((4, points), jnp.float32),
        in_specs=[pl.BlockSpec(memory_space=pltpu.VMEM)] * (len(hints) + 6),
        out_specs=pl.BlockSpec(memory_space=pltpu.VMEM),
        scratch_shapes=[
            pltpu.VMEM((radix * rows, 2 * LANES), jnp.float32),
        ],
        compiler_params=pltpu.CompilerParams(vmem_limit_bytes=16 * MIB),
        cost_estimate=pl.CostEstimate(
            flops=6 * radix * rows * 256 * 256, bytes_accessed=24 * rows * points, transcendentals=0
        ),
    )(*hints, *tables, cipher, total)


def xor_pairs(size, step):
    return [(i, i ^ step) for i in range(size)]


def sum_over(x, axis):
    size = lax.axis_size(axis)
    if size == 4:
        near, far, across = [lax.ppermute(x, axis, xor_pairs(size, step)) for step in (1, 2, 3)]
        return (x + near) + (far + across)
    if size & (size - 1):
        return lax.psum(x, axis)
    step = 1
    while step < size:
        x = x + lax.ppermute(x, axis, xor_pairs(size, step))
        step *= 2
    return x


def line_total(lwe, database, cipher, tables, total):
    own = cipher.shape[1]
    q = own // 4
    h = own - q
    (first,), (far_mid, far_tail) = line_hint(lwe, database, [(0, 3), (1, 1)], [[(0, own)], [(0, h), (h, q)]], 56)
    near = lax.ppermute(first, "col", NEIGHBOURS)
    cross = lax.ppermute(far_mid, "col", CROSS)
    direct = lax.ppermute(far_mid, "col", END_TO_FAR_MIDDLE)
    lwe, database, cipher = lax.optimization_barrier((lwe, database, cipher, first))[:3]
    (kept,), (later,) = line_hint(lwe, database, [(3, 2), (2, 0)], [[(0, own)]] * 2, 32)
    cuts = [(0, 2 * q), (2 * q, q), (h, q)]
    swapped = [swap_digits(cipher, top, rows) for top, rows in cuts]
    near, kept, swapped = lax.optimization_barrier((near, kept, swapped))
    end = at_end()
    round_a = lax.ppermute(later[: 2 * q] + jnp.where(end, 0.0, near[: 2 * q]), "col", ROUND)
    spare = jnp.where(end, far_tail, later[h:] + near[h:])
    piece = later[2 * q : h] + jnp.where(end, 0.0, near[2 * q : h])
    round_b = lax.ppermute(jnp.concatenate([piece, spare], axis=0), "col", ROUND)
    near_tail = lax.ppermute(later[h:], "col", INWARD)
    far_sum = lax.ppermute(far_tail + round_b[q:], "col", CROSS)
    base = kept + jnp.where(end, near, 0.0)
    hint_a = base[: 2 * q] + (cross[: 2 * q] + direct[: 2 * q]) + round_a
    waited, _ = lax.optimization_barrier((round_b, hint_a))
    hint_b = base[2 * q : h] + (cross[2 * q :] + direct[2 * q :]) + waited[:q]
    far_sum, _ = lax.optimization_barrier((far_sum, hint_b))
    with_a = lambda t: transform_products([hint_a, lax.ppermute(hint_a, "row", SWAP)], tables, swapped[0], t)
    total = with_a(total)
    far_sum, total = lax.optimization_barrier((far_sum, total))
    hint_c = base[h:] + jnp.where(end, round_b[q:], 0.0) + (near_tail + far_sum)
    for hint, part in ((hint_b, swapped[1]), (hint_c, swapped[2])):
        total = transform_products([hint, lax.ppermute(hint, "row", SWAP)], tables, part, total)
    return total


def body(parts, database, lwe_matrix, secret_ct):
    row_count, row_rank = lax.axis_size("row"), lax.axis_index("row")
    col_count = lax.axis_size("col")
    points = database.shape[0]
    degree = points * row_count
    radix = points // LANES
    own = secret_ct.shape[3]

    source = (row_rank + jnp.arange(row_count, dtype=jnp.int32)) % row_count if row_count == 2 else jnp.arange(row_count, dtype=jnp.int32)
    index = (source[:, None] * points + jnp.arange(points, dtype=jnp.int32)[None, :]) * (2 * row_rank + 1) % (2 * degree)
    angle = index.astype(jnp.float32) * (np.pi / degree)
    first = jnp.stack([jnp.cos(angle), -jnp.sin(angle)], axis=1).reshape(2 * row_count, points)
    lane = np.arange(LANES)
    turn = 2 * np.pi * (np.arange(radix)[:, None] * lane[None, :] % points) / points
    twist = jnp.asarray(np.stack([np.cos(turn), np.sin(turn)], axis=1).reshape(2 * radix, LANES), jnp.float32)
    small = 2 * np.pi * (lane[:, None] * lane[None, :] % LANES) / LANES
    table = np.block([[np.cos(small), -np.sin(small)], [np.sin(small), np.cos(small)]]).astype(np.float32)
    high = table.astype(jnp.bfloat16)
    low = (table - high.astype(np.float32)).astype(jnp.bfloat16)
    tables = (first, twist, jnp.asarray(high), jnp.asarray(low))

    lwe = lwe_matrix[:, 0, :]
    cipher = secret_ct.reshape(4, own, points)
    total = jnp.zeros((4, points), jnp.float32)
    if col_count == 4 and row_count == 2 and own == LANES and points % 512 == 0:
        total = line_total(lwe, database, cipher, tables, total)
    else:
        swapped = cipher.reshape(4, own, LANES, radix).swapaxes(2, 3).reshape(4, own, points)
        partial = partial_hint(lwe, database, col_count, parts)
        block = own // parts
        for k in range(parts):
            mine = lax.psum_scatter(partial[k], "col", scatter_dimension=0, tiled=True)
            if row_count == 2:
                hints = [mine, lax.ppermute(mine, "row", SWAP)]
            else:
                gathered = lax.all_gather(mine, "row")
                hints = [gathered[b] for b in range(row_count)]
            total = transform_products(hints, tables, swapped[:, k * block : (k + 1) * block], total)
    total = sum_over(sum_over(total, "limb"), "col")
    scale = 1.0 / (math.sqrt(degree) * math.sqrt(2 * lwe_matrix.shape[2]))
    total = total.reshape(4, radix, LANES).swapaxes(1, 2).reshape(2, 2, points)
    return total * scale


def solution(mesh):
    placed = (P(("grp", "row"), "col"), P("col", "limb", None), P(None, None, "limb", "col", "row"))

    def whole(database, lwe_matrix, secret_ct):
        own = lwe_matrix.shape[2] // mesh.shape["col"]
        parts = 2 if own % 16 == 0 else 1
        return jax.shard_map(
            functools.partial(body, parts), mesh=mesh, in_specs=placed, out_specs=P("grp", None, "row"), check_vma=False
        )(database, lwe_matrix, secret_ct)

    return whole
```
